32 devices in a mesh: seq: 8 (over z, y), mp: 4 (over x, core).
Axes of the slice: x: 2, y: 2, z: 4, core: 2. Of those that a mesh axis runs over, the one named last changes fastest.
Arguments:
- tokens: bfloat16 [1024, 8192], P('seq', 'mp'), may hold values from -6 to 6
- in_weight: bfloat16 [8192, 3, 4096], P('seq', None, 'mp'), may hold values from -0.0625 to 0.0625
- short_taps: float32 [3, 3, 4096], P(None, None, 'mp'), may hold values from -4 to 4
- carry_rows: bfloat16 [2, 3, 4096], P(None, None, 'mp'), may hold values from -6 to 6
- pole_rates: float32 [16, 16], replicated, may hold values from 3e-05 to 0.03
- residues: float32 [16, 16], replicated, may hold values from -0.1 to 0.1
- carry_state: float32 [4096, 16], P('mp'), may hold values from -60 to 60
- skip_gain: float32 [4096], P('mp'), may hold values from -4 to 4
- groups: int32 [4096], P('mp'), may hold values from 0 to 15
Outputs:
- result: bfloat16 [1024, 4096], P('seq', 'mp')
The draws below stay inside these ranges and needn't reach their ends.
All inputs are finite; a program needn't handle non-finite values.
Results may differ from the reference program's by a relative error of at most 0.008.
Values may be sent and summed in bfloat16 or wider, within the bound.
No kernel may reach another device: no remote copies, remote signals or barrier semaphores. Data moves between devices by JAX's collectives and lax.ppermute only.
A program may use at most 128 MiB of HBM per device.

```python
import math
import jax
import jax.numpy as jnp
from jax import lax

D = 8192
C = 4096
G = 16
ORDER = 16
TAPS = 3
LEN = 1024


def plant(array, rng, least, top_value):
    longest = array.shape.index(max(array.shape))
    spots = []
    for shift in (0, 1):
        where = [jax.random.randint(jax.random.fold_in(rng, axis), (), 0, length) for axis, length in enumerate(array.shape)]
        where[longest] = (where[longest] + shift) % array.shape[longest]
        spots.append(tuple(where))
    return array.at[spots[0]].set(least).at[spots[1]].set(top_value)


def steps_of(key, dims, shards, smallest, largest):
    factor_of, own = 1.0, jax.random.fold_in(key, 6)
    for axis_at, shards_of in shards:
        heights = jnp.exp(jax.random.uniform(jax.random.fold_in(own, axis_at), (shards_of,), jnp.float32, smallest / len(shards), largest / len(shards)))
        factor_of = factor_of * jnp.repeat(heights, dims[axis_at] // shards_of).reshape([-1 if axis == axis_at else 1 for axis in range(len(dims))])
    return factor_of


def noise(key, dims, scale, limit, cuts=(), held_as=jnp.bfloat16):
    drawn = jax.random.normal(key, dims, jnp.float32) * scale
    if len(cuts) > 0:
        drawn = steps_of(key, dims, cuts, -0.22, 0.18) * drawn
    return jnp.clip(drawn, min=-limit, max=limit).astype(held_as)


def setup_inputs(seed: int = 0) -> dict:
    splits = jax.random.split(jax.random.key(seed), 10)
    return {
        "tokens": noise(splits[0], (LEN, D), 1.0, 6.0, ((0, 8), (1, 4))),
        "in_weight": noise(splits[1], (D, 3, C), D ** -0.5, 0.0625, ((0, 8), (2, 4))),
        "short_taps": noise(splits[2], (TAPS, 3, C), 0.8, 4.0, ((2, 4),), jnp.float32),
        "carry_rows": noise(splits[3], (TAPS - 1, 3, C), 1.0, 6.0, ((2, 4),)),
        "pole_rates": jnp.clip(jnp.exp(jax.random.uniform(splits[4], (G, ORDER), jnp.float32, math.log(2.9999999242136255e-05), math.log(0.03))), 2.9999999242136255e-05, 0.03),
        "residues": noise(splits[5], (G, ORDER), 0.02, 0.1, (), jnp.float32),
        "carry_state": noise(splits[6], (C, ORDER), 10.0, 60.0, ((0, 4),), jnp.float32),
        "skip_gain": noise(splits[7], (C,), 1.0, 4.0, ((0, 4),), jnp.float32),
        "groups": plant(jax.random.randint(splits[8], (C,), 0, G), jax.random.fold_in(splits[8], 1), 0, G - 1).astype(jnp.int32),
    }


def reference(tokens, in_weight, short_taps, carry_rows, pole_rates, residues, carry_state, skip_gain, groups):
    highest = lax.Precision.HIGHEST
    projected = jnp.dot(tokens, in_weight.reshape(D, 3 * C), preferred_element_type=jnp.float32)
    projected = projected.astype(jnp.bfloat16).reshape(LEN, 3, C)
    extended = jnp.concatenate([carry_rows, projected], axis=0).astype(jnp.float32)
    short_mix = short_taps[0] * extended[2:] + short_taps[1] * extended[1:-1] + short_taps[2] * extended[:-2]
    query_rows = short_mix[:, 0]
    gated_rows = (short_mix[:, 1] * short_mix[:, 2]).astype(jnp.bfloat16)
    one_hot = (groups[:, None] == jnp.arange(G, dtype=jnp.int32)[None, :]).astype(jnp.float32)
    chan_res = jnp.dot(one_hot, residues, precision=highest)
    positions = jnp.arange(LEN).astype(jnp.float32)
    group_kernel = jnp.sum(residues[:, :, None] * jnp.exp(-pole_rates[:, :, None] * positions), axis=1)
    kernel = jnp.dot(one_hot, group_kernel, precision=highest)
    signal = gated_rows.astype(jnp.float32).T
    spectrum = jnp.fft.rfft(signal, n=2 * LEN, axis=1) * jnp.fft.rfft(kernel, n=2 * LEN, axis=1)
    conv_long = jnp.fft.irfft(spectrum, n=2 * LEN, axis=1)[:, :LEN]
    weights_mix = (one_hot[:, :, None] * (chan_res * carry_state)[:, None, :]).reshape(C, G * ORDER)
    decay_table = jnp.exp(-pole_rates[:, :, None] * (positions + 1.0)).reshape(G * ORDER, LEN)
    carried_part = jnp.dot(weights_mix, decay_table, precision=highest)
    long_mixed = (conv_long + carried_part).astype(jnp.bfloat16)
    long_mixed = lax.optimization_barrier(long_mixed)
    result = query_rows * (long_mixed.T.astype(jnp.float32) + skip_gain * gated_rows.astype(jnp.float32))
    return result.astype(jnp.bfloat16)
```

```python
import functools

import jax
import jax.numpy as jnp
from jax import lax
from jax.experimental import pallas as pl
from jax.experimental.pallas import tpu as pltpu
from jax.sharding import PartitionSpec as P

LANES = 128
SUBLANES = 8


def mode_scan(
    order,
    own_q,
    own_k,
    own_v,
    up_q,
    up_k,
    up_v,
    down_q,
    down_k,
    down_v,
    taps,
    carry,
    decay,
    decay_chunk,
    weight,
    state,
    skip,
    out,
    ext,
    query,
    gated,
    mixed,
    ends,
    starts,
):
    length = query.shape[0]
    rows = length // len(order)
    steps = length // SUBLANES
    modes = decay.shape[0]
    f32 = jnp.float32
    branches = ((own_q, up_q, down_q), (own_k, up_k, down_k), (own_v, up_v, down_v))
    for j, (own, up, down) in enumerate(branches):
        ext[j, SUBLANES - 2 : SUBLANES, :] = carry[:, j, :].astype(f32)
        for t, place in enumerate(order):
            src = pl.ds(place * rows, rows)
            total = own[src, :] + up[src, :].astype(f32) + down[src, :].astype(f32)
            ext[j, pl.ds(SUBLANES + t * rows, rows), :] = total.astype(jnp.bfloat16).astype(f32)
    for t in range(len(order)):
        mix = []
        for j in range(3):
            acc = taps[0, j : j + 1, :] * ext[j, pl.ds(SUBLANES + t * rows, rows), :]
            acc = acc + taps[1, j : j + 1, :] * ext[j, pl.ds(SUBLANES - 1 + t * rows, rows), :]
            acc = acc + taps[2, j : j + 1, :] * ext[j, pl.ds(SUBLANES - 2 + t * rows, rows), :]
            mix.append(acc)
        query[pl.ds(t * rows, rows), :] = mix[0]
        gated[pl.ds(t * rows, rows), :] = (mix[1] * mix[2]).astype(jnp.bfloat16).astype(f32)

    lanes = query.shape[1]
    rates = [jnp.broadcast_to(decay[r : r + 1, :], (SUBLANES, lanes)) for r in range(modes)]

    def advance(i, held):
        x = gated[pl.ds(i, SUBLANES, stride=steps), :]
        return tuple(a * s + x for a, s in zip(rates, held))

    zero = jnp.zeros((SUBLANES, lanes), f32)
    held = lax.fori_loop(0, steps, advance, (zero,) * modes, unroll=8)
    for r in range(modes):
        ends[r] = held[r]
    start = state[...]
    for n in range(SUBLANES):
        starts[:, n, :] = start
        start = decay_chunk[...] * start + ends[:, n, :]

    weights = [jnp.broadcast_to(weight[r : r + 1, :], (SUBLANES, lanes)) for r in range(modes)]

    def emit(i, held):
        x = gated[pl.ds(i, SUBLANES, stride=steps), :]
        held = tuple(a * s + x for a, s in zip(rates, held))
        terms = [w * s for w, s in zip(weights, held)]
        while len(terms) > 1:
            terms = [sum(terms[k : k + 2]) for k in range(0, len(terms), 2)]
        mixed[pl.ds(i, SUBLANES, stride=steps), :] = terms[0]
        return held

    lax.fori_loop(0, steps, emit, tuple(starts[r] for r in range(modes)), unroll=8)
    for t in range(len(order)):
        at = pl.ds(t * rows, rows)
        long_rows = mixed[at, :].astype(jnp.bfloat16).astype(f32)
        out[at, :] = (query[at, :] * (long_rows + skip[...] * gated[at, :])).astype(jnp.bfloat16)


def run_mode_scan(order, sums, taps, carry, decay, decay_chunk, weight, state, skip):
    length, width = sums[0].shape
    lanes = -(-width // LANES) * LANES
    operands = [*sums, taps, carry, decay, decay_chunk, weight, state, skip]
    if lanes != width:
        operands = [
            jnp.pad(x, [(0, 0)] * (x.ndim - 1) + [(0, lanes - width)]) for x in operands
        ]
    modes = decay.shape[0]
    f32 = jnp.float32
    out = pl.pallas_call(
        functools.partial(mode_scan, order),
        out_shape=jax.ShapeDtypeStruct((length, lanes), jnp.bfloat16),
        in_specs=[pl.BlockSpec(memory_space=pltpu.VMEM)] * len(operands),
        out_specs=pl.BlockSpec(memory_space=pltpu.VMEM),
        scratch_shapes=[
            pltpu.VMEM((3, length + SUBLANES, lanes), f32),
            pltpu.VMEM((length, lanes), f32),
            pltpu.VMEM((length, lanes), f32),
            pltpu.VMEM((length, lanes), f32),
            pltpu.VMEM((modes, SUBLANES, lanes), f32),
            pltpu.VMEM((modes, SUBLANES, lanes), f32),
        ],
        compiler_params=pltpu.CompilerParams(vmem_limit_bytes=48 * 2**20),
        cost_estimate=pl.CostEstimate(
            flops=6 * modes * length * lanes, bytes_accessed=40 * length * lanes, transcendentals=0
        ),
    )(*operands)
    return out[:, :width]


def channel_modes(chan_groups, pole_rates, residues):
    highest = lax.Precision.HIGHEST
    one_hot = (
        jnp.arange(pole_rates.shape[0], dtype=jnp.int32)[:, None] == chan_groups[None, :]
    ).astype(jnp.float32)
    chan_rates = jnp.dot(pole_rates.T, one_hot, precision=highest)
    chan_res = jnp.dot(residues.T, one_hot, precision=highest)
    return (chan_rates, chan_res)


def line_sums(partial, line, at, width):
    f32, length = jnp.float32, partial.shape[0]

    def block(index):
        index = jnp.clip(index, 0, line - 1)
        return lax.dynamic_slice(partial, (0, index * width), (length, width))

    up = down = None
    for k in range(1, line):
        out_up, out_down = block(at + line - k), block(at - line + k)
        if k > 1:
            out_up = out_up + up.astype(f32)
            out_down = out_down + down.astype(f32)
        pairs = [(2 * z + y, 2 * z + 2 + y) for z in range(k) for y in range(2)]
        last = 2 * line - 1
        mirrored = [(last - i, last - j) for i, j in pairs]
        up = lax.ppermute(out_up.astype(jnp.bfloat16), "seq", pairs)
        down = lax.ppermute(out_down.astype(jnp.bfloat16), "seq", mirrored)
    return block(at), up, down


def shards(
    tokens, in_weight, short_taps, carry_rows, pole_rates, residues, carry_state, skip_gain, groups
):
    f32 = jnp.float32
    seq, mp = lax.axis_size("seq"), lax.axis_size("mp")
    line = seq // 2
    here = lax.axis_index("seq")
    at, side = here // 2, here % 2
    depth, _, columns = in_weight.shape
    assert seq % 2 == 0 and line == mp and tokens.shape[1] == 2 * depth
    width = columns // seq
    half = columns // 2

    by_branch = in_weight.transpose(1, 0, 2)
    away = lax.dynamic_slice(by_branch, (0, 0, (1 - side) * half), (3, depth, half))
    kept = lax.dynamic_slice(by_branch, (0, 0, side * half), (3, depth, half))
    swap = [(i, i ^ 1) for i in range(seq)]
    arrived = [lax.ppermute(away[j], "seq", swap) for j in range(3)]

    turn = [
        ((2 * z + y) * mp + m, (2 * m + y) * mp + z)
        for z in range(line)
        for y in range(2)
        for m in range(mp)
    ]
    turned = lax.ppermute(tokens, ("seq", "mp"), turn)
    planes = [[z * 2 * mp + i for i in range(2 * mp)] for z in range(line)]
    rows = lax.all_gather(turned, ("seq", "mp"), axis=0, tiled=True, axis_index_groups=planes)
    length = rows.shape[0]
    rows_kept = lax.dynamic_slice(rows, (0, side * depth), (length, depth))
    rows_other = lax.dynamic_slice(rows, (0, (1 - side) * depth), (length, depth))

    sums = []
    for j in range(3):
        partial = jnp.dot(rows_kept, kept[j], preferred_element_type=f32) + jnp.dot(
            rows_other, arrived[j], preferred_element_type=f32
        )
        sums.append(line_sums(partial, line, at, width))
    sums = [sums[j][k] for k in range(3) for j in range(3)]

    first = (side * line + at) * width

    def own(array, axis):
        return lax.dynamic_slice_in_dim(array, first, width, axis)

    chan_rates, chan_res = channel_modes(own(groups, 0), pole_rates, residues)
    order = tuple((t % 2) * mp + t // 2 for t in range(seq))
    mixed = run_mode_scan(
        order,
        sums,
        own(short_taps, 2),
        own(carry_rows, 2),
        jnp.exp(-chan_rates),
        jnp.exp(-chan_rates * (length // SUBLANES)),
        chan_res,
        own(carry_state.T, 1),
        own(skip_gain, 0)[None, :],
    )
    back = lax.all_to_all(
        mixed.reshape(seq, length // seq, width), "seq", split_axis=0, concat_axis=0, tiled=True
    )
    back = back.reshape(line, 2, length // seq, width).transpose(2, 1, 0, 3)
    return back.reshape(length // seq, columns)


def solution(mesh):
    in_specs = (
        P("seq", "mp"),
        P("seq", None, "mp"),
        P(None, None, "mp"),
        P(None, None, "mp"),
        P(),
        P(),
        P("mp", None),
        P("mp"),
        P("mp"),
    )
    out_specs = P("seq", "mp")
    return jax.shard_map(shards, mesh=mesh, in_specs=in_specs, out_specs=out_specs, check_vma=False)
```

```python
import jax
import jax.numpy as jnp
from jax import lax
from jax.experimental import pallas as pl
from jax.experimental.pallas import tpu as pltpu
from jax.sharding import PartitionSpec as P

LANES = 128
SUBLANES = 8


def mode_scan(token_at, *refs):
    *sums, taps, carry, decay, decay_chunk, weight, state, skip = refs[:-7]
    out, ext, query, gated, mixed, ends, starts = refs[-7:]
    length = query.shape[0]
    blocks = token_at.shape[0]
    rows = length // blocks
    steps = length // SUBLANES
    modes = decay.shape[0]
    f32 = jnp.float32
    parts = len(sums) // 6
    for j in range(3):
        ext[j, SUBLANES - 2 : SUBLANES, :] = carry[:, j, :].astype(f32)
    for p in range(blocks):
        part, place = divmod(p, blocks // parts)
        src = pl.ds(place * rows, rows)
        dst = pl.ds(pl.multiple_of(token_at[p] * rows + SUBLANES, SUBLANES), rows)
        for j in range(3):
            own, other = sums[2 * (3 * part + j)], sums[2 * (3 * part + j) + 1]
            total = own[src, :] + other[src, :].astype(f32)
            ext[j, dst, :] = total.astype(jnp.bfloat16).astype(f32)
    for t in range(blocks):
        mix = []
        for j in range(3):
            acc = taps[0, j : j + 1, :] * ext[j, pl.ds(SUBLANES + t * rows, rows), :]
            acc = acc + taps[1, j : j + 1, :] * ext[j, pl.ds(SUBLANES - 1 + t * rows, rows), :]
            acc = acc + taps[2, j : j + 1, :] * ext[j, pl.ds(SUBLANES - 2 + t * rows, rows), :]
            mix.append(acc)
        query[pl.ds(t * rows, rows), :] = mix[0]
        gated[pl.ds(t * rows, rows), :] = (mix[1] * mix[2]).astype(jnp.bfloat16).astype(f32)

    lanes = query.shape[1]
    rates = [jnp.broadcast_to(decay[r : r + 1, :], (SUBLANES, lanes)) for r in range(modes)]

    def advance(i, held):
        x = gated[pl.ds(i, SUBLANES, stride=steps), :]
        return tuple(a * s + x for a, s in zip(rates, held))

    zero = jnp.zeros((SUBLANES, lanes), f32)
    held = lax.fori_loop(0, steps, advance, (zero,) * modes, unroll=8)
    for r in range(modes):
        ends[r] = held[r]
    start = state[...]
    for n in range(SUBLANES):
        starts[:, n, :] = start
        start = decay_chunk[...] * start + ends[:, n, :]

    weights = [jnp.broadcast_to(weight[r : r + 1, :], (SUBLANES, lanes)) for r in range(modes)]

    def emit(i, held):
        x = gated[pl.ds(i, SUBLANES, stride=steps), :]
        held = tuple(a * s + x for a, s in zip(rates, held))
        terms = [w * s for w, s in zip(weights, held)]
        while len(terms) > 1:
            terms = [sum(terms[k : k + 2]) for k in range(0, len(terms), 2)]
        mixed[pl.ds(i, SUBLANES, stride=steps), :] = terms[0]
        return held

    lax.fori_loop(0, steps, emit, tuple(starts[r] for r in range(modes)), unroll=8)
    for t in range(blocks):
        at = pl.ds(t * rows, rows)
        long_rows = mixed[at, :].astype(jnp.bfloat16).astype(f32)
        out[at, :] = (query[at, :] * (long_rows + skip[...] * gated[at, :])).astype(jnp.bfloat16)


def run_mode_scan(token_at, sums, taps, carry, decay, decay_chunk, weight, state, skip):
    blocks = token_at.shape[0]
    width = sums[0].shape[1]
    length = sum(x.shape[0] for x in sums[::6])
    lanes = -(-width // LANES) * LANES
    operands = [*sums, taps, carry, decay, decay_chunk, weight, state, skip]
    if lanes != width:
        operands = [
            jnp.pad(x, [(0, 0)] * (x.ndim - 1) + [(0, lanes - width)]) for x in operands
        ]
    modes = decay.shape[0]
    f32 = jnp.float32
    out = pl.pallas_call(
        mode_scan,
        out_shape=jax.ShapeDtypeStruct((length, lanes), jnp.bfloat16),
        in_specs=[pl.BlockSpec(memory_space=pltpu.SMEM)]
        + [pl.BlockSpec(memory_space=pltpu.VMEM)] * len(operands),
        out_specs=pl.BlockSpec(memory_space=pltpu.VMEM),
        scratch_shapes=[
            pltpu.VMEM((3, length + SUBLANES, lanes), f32),
            pltpu.VMEM((length, lanes), f32),
            pltpu.VMEM((length, lanes), f32),
            pltpu.VMEM((length, lanes), f32),
            pltpu.VMEM((modes, SUBLANES, lanes), f32),
            pltpu.VMEM((modes, SUBLANES, lanes), f32),
        ],
        compiler_params=pltpu.CompilerParams(vmem_limit_bytes=48 * 2**20),
        cost_estimate=pl.CostEstimate(
            flops=6 * modes * length * lanes, bytes_accessed=40 * length * lanes, transcendentals=0
        ),
    )(token_at, *operands)
    return out[:, :width]


def channel_modes(chan_groups, pole_rates, residues):
    highest = lax.Precision.HIGHEST
    one_hot = (
        jnp.arange(pole_rates.shape[0], dtype=jnp.int32)[:, None] == chan_groups[None, :]
    ).astype(jnp.float32)
    chan_rates = jnp.dot(pole_rates.T, one_hot, precision=highest)
    chan_res = jnp.dot(residues.T, one_hot, precision=highest)
    return (chan_rates, chan_res)


def bits_turned(index, count):
    turned, bit = index * 0, 1
    while bit < count:
        turned = turned * 2 + index // bit % 2
        bit *= 2
    return turned


def swapped(array, axis, bit):
    return lax.ppermute(array, axis, [(i, i ^ bit) for i in range(lax.axis_size(axis))])


def halves(array, axis, upper):
    half = array.shape[axis] // 2
    stays = lax.dynamic_slice_in_dim(array, upper * half, half, axis)
    goes = lax.dynamic_slice_in_dim(array, (1 - upper) * half, half, axis)
    return stays, goes


def plane_rows(turned):
    pieces = [turned]
    pieces = pieces + [swapped(turned, "seq", 1)]
    crossed = pieces[1]
    bit = lax.axis_size("mp") // 2
    while bit:
        pieces = pieces + [swapped(piece, "mp", bit) for piece in pieces]
        bit //= 2
    return pieces, crossed


def shards(
    tokens, in_weight, short_taps, carry_rows, pole_rates, residues, carry_state, skip_gain, groups
):
    f32, bf16 = jnp.float32, jnp.bfloat16
    seq, mp = lax.axis_size("seq"), lax.axis_size("mp")
    line = seq // 2
    here, shard = lax.axis_index("seq"), lax.axis_index("mp")
    side = here % 2
    depth, _, columns = in_weight.shape
    assert seq & (seq - 1) == 0 and line == mp and tokens.shape[1] == 2 * depth
    width = columns // seq

    turn = [
        ((2 * z + y) * mp + m, (2 * m + y) * mp + bits_turned(z, line))
        for z in range(line)
        for y in range(2)
        for m in range(mp)
    ]
    turned = lax.ppermute(tokens, ("seq", "mp"), turn)

    by_branch = in_weight.transpose(1, 0, 2)
    kept, away = zip(*(halves(by_branch[j], 1, side) for j in range(3)))
    arrived = [swapped(away[0], "seq", 1)]
    pieces, crossed = plane_rows(turned)
    later = lax.optimization_barrier((away[1], away[2], crossed))
    arrived = arrived + [swapped(later[j], "seq", 1) for j in range(2)]

    chunks = [pieces[: seq // 2], pieces[seq // 2 :]]
    chunks = [jnp.concatenate(chunk, axis=0) for chunk in chunks]
    split = [halves(chunk, 1, side) for chunk in chunks]

    sums = {}
    for j in range(3):
        for part, (rows_kept, rows_other) in enumerate(split):
            total = jnp.dot(rows_kept, kept[j], preferred_element_type=f32) + jnp.dot(
                rows_other, arrived[j], preferred_element_type=f32
            )
            bit = 2
            while bit < seq:
                total, goes = halves(total, 1, here // bit % 2)
                came = swapped(goes.astype(bf16), "seq", bit)
                bit *= 2
                if bit < seq:
                    total = total + came.astype(f32)
            sums[part, j] = (total, came)
    sums = [term for part in range(2) for j in range(3) for term in sums[part, j]]

    first = bits_turned(here, seq) * width

    def own(array, axis):
        return lax.dynamic_slice_in_dim(array, first, width, axis)

    length = tokens.shape[0] * seq
    chan_rates, chan_res = channel_modes(own(groups, 0), pole_rates, residues)
    places = jnp.arange(seq, dtype=jnp.int32)
    holder = shard ^ bits_turned(places // 2, mp)
    token_at = 2 * bits_turned(holder, mp) + (side ^ (places % 2))
    mixed = run_mode_scan(
        token_at.astype(jnp.int32),
        sums,
        own(short_taps, 2),
        own(carry_rows, 2),
        jnp.exp(-chan_rates),
        jnp.exp(-chan_rates * (length // SUBLANES)),
        chan_res,
        own(carry_state.T, 1),
        own(skip_gain, 0)[None, :],
    )
    back = lax.all_to_all(
        mixed.reshape(seq, length // seq, width), "seq", split_axis=0, concat_axis=0, tiled=True
    )
    return jnp.concatenate([back[bits_turned(i, seq)] for i in range(seq)], axis=1)


def solution(mesh):
    in_specs = (
        P("seq", "mp"),
        P("seq", None, "mp"),
        P(None, None, "mp"),
        P(None, None, "mp"),
        P(),
        P(),
        P("mp", None),
        P("mp"),
        P("mp"),
    )
    out_specs = P("seq", "mp")
    return jax.shard_map(shards, mesh=mesh, in_specs=in_specs, out_specs=out_specs, check_vma=False)
```

```python
import jax
import jax.numpy as jnp
from jax import lax
from jax.experimental import pallas as pl
from jax.experimental.pallas import tpu as pltpu
from jax.sharding import PartitionSpec as P

LANES = 128
SUBLANES = 8


def mode_scan(token_at, *refs):
    *sums, taps, carry, decay, decay_chunk, weight, state, skip = refs[:-7]
    out, ext, query, gated, mixed, ends, starts = refs[-7:]
    length = query.shape[0]
    blocks = token_at.shape[0]
    rows = length // blocks
    steps = length // SUBLANES
    modes = decay.shape[0]
    f32 = jnp.float32
    parts = len(sums) // 6
    for j in range(3):
        ext[j, SUBLANES - 2 : SUBLANES, :] = carry[:, j, :].astype(f32)
    for p in range(blocks):
        part, place = divmod(p, blocks // parts)
        src = pl.ds(place * rows, rows)
        dst = pl.ds(pl.multiple_of(token_at[p] * rows + SUBLANES, SUBLANES), rows)
        for j in range(3):
            own, other = sums[2 * (3 * part + j)], sums[2 * (3 * part + j) + 1]
            total = own[src, :] + other[src, :].astype(f32)
            ext[j, dst, :] = total.astype(jnp.bfloat16).astype(f32)
    for t in range(blocks):
        mix = []
        for j in range(3):
            acc = taps[0, j : j + 1, :] * ext[j, pl.ds(SUBLANES + t * rows, rows), :]
            acc = acc + taps[1, j : j + 1, :] * ext[j, pl.ds(SUBLANES - 1 + t * rows, rows), :]
            acc = acc + taps[2, j : j + 1, :] * ext[j, pl.ds(SUBLANES - 2 + t * rows, rows), :]
            mix.append(acc)
        query[pl.ds(t * rows, rows), :] = mix[0]
        gated[pl.ds(t * rows, rows), :] = (mix[1] * mix[2]).astype(jnp.bfloat16).astype(f32)

    lanes = query.shape[1]
    rates = [jnp.broadcast_to(decay[r : r + 1, :], (SUBLANES, lanes)) for r in range(modes)]

    def advance(i, held):
        x = gated[pl.ds(i, SUBLANES, stride=steps), :]
        return tuple(a * s + x for a, s in zip(rates, held))

    zero = jnp.zeros((SUBLANES, lanes), f32)
    held = lax.fori_loop(0, steps, advance, (zero,) * modes, unroll=8)
    for r in range(modes):
        ends[r] = held[r]
    start = state[...]
    for n in range(SUBLANES):
        starts[:, n, :] = start
        start = decay_chunk[...] * start + ends[:, n, :]

    weights = [jnp.broadcast_to(weight[r : r + 1, :], (SUBLANES, lanes)) for r in range(modes)]

    def emit(i, held):
        x = gated[pl.ds(i, SUBLANES, stride=steps), :]
        held = tuple(a * s + x for a, s in zip(rates, held))
        terms = [w * s for w, s in zip(weights, held)]
        while len(terms) > 1:
            terms = [sum(terms[k : k + 2]) for k in range(0, len(terms), 2)]
        mixed[pl.ds(i, SUBLANES, stride=steps), :] = terms[0]
        return held

    lax.fori_loop(0, steps, emit, tuple(starts[r] for r in range(modes)), unroll=8)
    for t in range(blocks):
        at = pl.ds(t * rows, rows)
        long_rows = mixed[at, :].astype(jnp.bfloat16).astype(f32)
        out[at, :] = (query[at, :] * (long_rows + skip[...] * gated[at, :])).astype(jnp.bfloat16)


def run_mode_scan(token_at, sums, taps, carry, decay, decay_chunk, weight, state, skip):
    blocks = token_at.shape[0]
    width = sums[0].shape[1]
    length = sum(x.shape[0] for x in sums[::6])
    lanes = -(-width // LANES) * LANES
    operands = [*sums, taps, carry, decay, decay_chunk, weight, state, skip]
    if lanes != width:
        operands = [
            jnp.pad(x, [(0, 0)] * (x.ndim - 1) + [(0, lanes - width)]) for x in operands
        ]
    modes = decay.shape[0]
    f32 = jnp.float32
    out = pl.pallas_call(
        mode_scan,
        out_shape=jax.ShapeDtypeStruct((length, lanes), jnp.bfloat16),
        in_specs=[pl.BlockSpec(memory_space=pltpu.SMEM)]
        + [pl.BlockSpec(memory_space=pltpu.VMEM)] * len(operands),
        out_specs=pl.BlockSpec(memory_space=pltpu.VMEM),
        scratch_shapes=[
            pltpu.VMEM((3, length + SUBLANES, lanes), f32),
            pltpu.VMEM((length, lanes), f32),
            pltpu.VMEM((length, lanes), f32),
            pltpu.VMEM((length, lanes), f32),
            pltpu.VMEM((modes, SUBLANES, lanes), f32),
            pltpu.VMEM((modes, SUBLANES, lanes), f32),
        ],
        compiler_params=pltpu.CompilerParams(vmem_limit_bytes=48 * 2**20),
        cost_estimate=pl.CostEstimate(
            flops=6 * modes * length * lanes, bytes_accessed=40 * length * lanes, transcendentals=0
        ),
    )(token_at, *operands)
    return out[:, :width]


def channel_modes(chan_groups, pole_rates, residues):
    highest = lax.Precision.HIGHEST
    one_hot = (
        jnp.arange(pole_rates.shape[0], dtype=jnp.int32)[:, None] == chan_groups[None, :]
    ).astype(jnp.float32)
    chan_rates = jnp.dot(pole_rates.T, one_hot, precision=highest)
    chan_res = jnp.dot(residues.T, one_hot, precision=highest)
    return (chan_rates, chan_res)


def bits_turned(index, count):
    turned, bit = index * 0, 1
    while bit < count:
        turned = turned * 2 + index // bit % 2
        bit *= 2
    return turned


def swapped(array, axis, bit):
    return lax.ppermute(array, axis, [(i, i ^ bit) for i in range(lax.axis_size(axis))])


def halves(array, axis, upper):
    half = array.shape[axis] // 2
    stays = lax.dynamic_slice_in_dim(array, upper * half, half, axis)
    goes = lax.dynamic_slice_in_dim(array, (1 - upper) * half, half, axis)
    return stays, goes


def plane_rows(halves_here):
    mp = lax.axis_size("mp")
    crossed = [swapped(half, "seq", 1) for half in halves_here][::-1]
    near = []
    for mine, other in zip(halves_here, crossed):
        pieces = [mine, other]
        bit = mp // 2
        while bit > 1:
            pieces = pieces + [swapped(piece, "mp", bit) for piece in pieces]
            bit //= 2
        near.append(jnp.concatenate(pieces, axis=0))
    far = [swapped(chunk, "mp", 1) for chunk in near]
    return [near, far], crossed


def shards(
    tokens, in_weight, short_taps, carry_rows, pole_rates, residues, carry_state, skip_gain, groups
):
    f32, bf16 = jnp.float32, jnp.bfloat16
    seq, mp = lax.axis_size("seq"), lax.axis_size("mp")
    line = seq // 2
    here, shard = lax.axis_index("seq"), lax.axis_index("mp")
    side = here % 2
    depth, _, columns = in_weight.shape
    assert seq & (seq - 1) == 0 and line == mp and tokens.shape[1] == 2 * depth
    width = columns // seq

    by_branch = in_weight.transpose(1, 0, 2)
    half = columns // 2

    def columns_of(weights, j, upper):
        return lax.dynamic_slice(weights, (j, 0, upper * half), (1, depth, half))[0]

    arrived = [swapped(columns_of(by_branch, 0, 1 - side), "seq", 1)]

    def turn(detour):
        return [
            ((2 * z + y) * mp + (m ^ detour), (2 * m + y) * mp + bits_turned(z, line))
            for z in range(line)
            for y in range(2)
            for m in range(mp)
        ]

    mine, other = halves(tokens, 1, side)
    hopped = swapped(other, "mp", mp // 2)
    turned = [
        lax.ppermute(mine, ("seq", "mp"), turn(0)),
        lax.ppermute(hopped, ("seq", "mp"), turn(mp // 2)),
    ]
    split, crossed = plane_rows(turned)
    by_branch, *_ = lax.optimization_barrier((by_branch, *crossed))
    arrived = arrived + [swapped(columns_of(by_branch, j, 1 - side), "seq", 1) for j in (1, 2)]
    kept = [columns_of(by_branch, j, side) for j in range(3)]

    sums, sent = [{}, {}], ()
    for j in range(3):
        came, *_ = lax.optimization_barrier((arrived[j], *sent))
        sent = ()
        for part, (rows_kept, rows_other) in enumerate(split):
            total = jnp.dot(rows_kept, kept[j], preferred_element_type=f32) + jnp.dot(
                rows_other, came, preferred_element_type=f32
            )
            bit = 2
            while bit < seq:
                total, goes = halves(total, 1, here // bit % 2)
                goes = goes.astype(bf16)
                other = swapped(goes, "seq", bit)
                bit *= 2
                if bit < seq:
                    total = total + other.astype(f32)
            sums[part][j] = (total, other)
            sent = (*sent, goes)
    sums = [term for part in sums for j in range(3) for term in part[j]]

    first = bits_turned(here, seq) * width

    def own(array, axis):
        return lax.dynamic_slice_in_dim(array, first, width, axis)

    length = tokens.shape[0] * seq
    chan_rates, chan_res = channel_modes(own(groups, 0), pole_rates, residues)
    places = jnp.arange(seq, dtype=jnp.int32)
    holder = shard ^ bits_turned(places // 2, mp)
    token_at = 2 * bits_turned(holder, mp) + (side ^ (places % 2))
    mixed = run_mode_scan(
        token_at.astype(jnp.int32),
        sums,
        own(short_taps, 2),
        own(carry_rows, 2),
        jnp.exp(-chan_rates),
        jnp.exp(-chan_rates * (length // SUBLANES)),
        chan_res,
        own(carry_state.T, 1),
        own(skip_gain, 0)[None, :],
    )
    back = lax.all_to_all(
        mixed.reshape(seq, length // seq, width), "seq", split_axis=0, concat_axis=0, tiled=True
    )
    bits = seq.bit_length() - 1
    back = back.reshape((2,) * bits + back.shape[1:])
    return back.transpose(bits, *range(bits)[::-1], bits + 1).reshape(length // seq, columns)


def solution(mesh):
    in_specs = (
        P("seq", "mp"),
        P("seq", None, "mp"),
        P(None, None, "mp"),
        P(None, None, "mp"),
        P(),
        P(),
        P("mp", None),
        P("mp"),
        P("mp"),
    )
    out_specs = P("seq", "mp")
    return jax.shard_map(shards, mesh=mesh, in_specs=in_specs, out_specs=out_specs, check_vma=False)
```

```python
import jax
import jax.numpy as jnp
from jax import lax
from jax.experimental import pallas as pl
from jax.experimental.pallas import tpu as pltpu
from jax.sharding import PartitionSpec as P

LANES = 128
SUBLANES = 8


def mode_scan(token_at, *refs):
    *sums, taps, carry, decay, decay_chunk, weight, state, skip = refs[:-7]
    out, ext, query, gated, mixed, ends, starts = refs[-7:]
    length = query.shape[0]
    blocks = token_at.shape[0]
    parts = len(sums) // 6
    rows = length // blocks
    share = rows // parts
    steps = length // SUBLANES
    modes = decay.shape[0]
    f32 = jnp.float32
    for j in range(3):
        ext[j, SUBLANES - 2 : SUBLANES, :] = carry[:, j, :].astype(f32)
    for part, p in [(part, p) for part in range(parts) for p in range(blocks)]:
        src = pl.ds(p * share, share)
        dst = pl.ds(
            pl.multiple_of(token_at[p] * rows + part * share + SUBLANES, SUBLANES), share
        )
        for j in range(3):
            own, other = sums[2 * (3 * part + j)], sums[2 * (3 * part + j) + 1]
            total = own[src, :] + other[src, :].astype(f32)
            ext[j, dst, :] = total.astype(jnp.bfloat16).astype(f32)
    for t in range(blocks):
        mix = []
        for j in range(3):
            acc = taps[0, j : j + 1, :] * ext[j, pl.ds(SUBLANES + t * rows, rows), :]
            acc = acc + taps[1, j : j + 1, :] * ext[j, pl.ds(SUBLANES - 1 + t * rows, rows), :]
            acc = acc + taps[2, j : j + 1, :] * ext[j, pl.ds(SUBLANES - 2 + t * rows, rows), :]
            mix.append(acc)
        query[pl.ds(t * rows, rows), :] = mix[0]
        gated[pl.ds(t * rows, rows), :] = (mix[1] * mix[2]).astype(jnp.bfloat16).astype(f32)

    lanes = query.shape[1]
    rates = [jnp.broadcast_to(decay[r : r + 1, :], (SUBLANES, lanes)) for r in range(modes)]

    def advance(i, held):
        x = gated[pl.ds(i, SUBLANES, stride=steps), :]
        return tuple(a * s + x for a, s in zip(rates, held))

    zero = jnp.zeros((SUBLANES, lanes), f32)
    held = lax.fori_loop(0, steps, advance, (zero,) * modes, unroll=8)
    for r in range(modes):
        ends[r] = held[r]
    start = state[...]
    for n in range(SUBLANES):
        starts[:, n, :] = start
        start = decay_chunk[...] * start + ends[:, n, :]

    weights = [jnp.broadcast_to(weight[r : r + 1, :], (SUBLANES, lanes)) for r in range(modes)]

    def emit(i, held):
        x = gated[pl.ds(i, SUBLANES, stride=steps), :]
        held = tuple(a * s + x for a, s in zip(rates, held))
        terms = [w * s for w, s in zip(weights, held)]
        while len(terms) > 1:
            terms = [sum(terms[k : k + 2]) for k in range(0, len(terms), 2)]
        mixed[pl.ds(i, SUBLANES, stride=steps), :] = terms[0]
        return held

    lax.fori_loop(0, steps, emit, tuple(starts[r] for r in range(modes)), unroll=8)
    for t in range(blocks):
        at = pl.ds(t * rows, rows)
        long_rows = mixed[at, :].astype(jnp.bfloat16).astype(f32)
        out[at, :] = (query[at, :] * (long_rows + skip[...] * gated[at, :])).astype(jnp.bfloat16)


def run_mode_scan(token_at, sums, taps, carry, decay, decay_chunk, weight, state, skip):
    blocks = token_at.shape[0]
    width = sums[0].shape[1]
    length = sum(x.shape[0] for x in sums[::6])
    lanes = -(-width // LANES) * LANES
    operands = [*sums, taps, carry, decay, decay_chunk, weight, state, skip]
    if lanes != width:
        operands = [
            jnp.pad(x, [(0, 0)] * (x.ndim - 1) + [(0, lanes - width)]) for x in operands
        ]
    modes = decay.shape[0]
    f32 = jnp.float32
    out = pl.pallas_call(
        mode_scan,
        out_shape=jax.ShapeDtypeStruct((length, lanes), jnp.bfloat16),
        in_specs=[pl.BlockSpec(memory_space=pltpu.SMEM)]
        + [pl.BlockSpec(memory_space=pltpu.VMEM)] * len(operands),
        out_specs=pl.BlockSpec(memory_space=pltpu.VMEM),
        scratch_shapes=[
            pltpu.VMEM((3, length + SUBLANES, lanes), f32),
            pltpu.VMEM((length, lanes), f32),
            pltpu.VMEM((length, lanes), f32),
            pltpu.VMEM((length, lanes), f32),
            pltpu.VMEM((modes, SUBLANES, lanes), f32),
            pltpu.VMEM((modes, SUBLANES, lanes), f32),
        ],
        compiler_params=pltpu.CompilerParams(vmem_limit_bytes=48 * 2**20),
        cost_estimate=pl.CostEstimate(
            flops=6 * modes * length * lanes, bytes_accessed=40 * length * lanes, transcendentals=0
        ),
    )(token_at, *operands)
    return out[:, :width]


def channel_modes(chan_groups, pole_rates, residues):
    highest = lax.Precision.HIGHEST
    one_hot = (
        jnp.arange(pole_rates.shape[0], dtype=jnp.int32)[:, None] == chan_groups[None, :]
    ).astype(jnp.float32)
    chan_rates = jnp.dot(pole_rates.T, one_hot, precision=highest)
    chan_res = jnp.dot(residues.T, one_hot, precision=highest)
    return (chan_rates, chan_res)


def bits_turned(index, count):
    turned, bit = index * 0, 1
    while bit < count:
        turned = turned * 2 + index // bit % 2
        bit *= 2
    return turned


def swapped(array, axis, bit):
    return lax.ppermute(array, axis, [(i, i ^ bit) for i in range(lax.axis_size(axis))])


def halves(array, axis, upper):
    half = array.shape[axis] // 2
    stays = lax.dynamic_slice_in_dim(array, upper * half, half, axis)
    goes = lax.dynamic_slice_in_dim(array, (1 - upper) * half, half, axis)
    return stays, goes


def picked(array, groups, upper):
    part = array.shape[1] // (2 * groups)
    starts = [(2 * g + upper) * part for g in range(groups)]
    return jnp.concatenate(
        [lax.dynamic_slice_in_dim(array, start, part, 1) for start in starts], axis=1
    )


def plane_rows(turned, crossed):
    pieces, bit = [turned, crossed], lax.axis_size("mp") // 2
    while bit > 1:
        pieces = pieces + [swapped(piece, "mp", bit) for piece in pieces]
        bit //= 2
    cut = turned.shape[1] // 2
    mine = [piece[:, cut:] if i % 2 else piece[:, :cut] for i, piece in enumerate(pieces)]
    other = [piece[:, :cut] if i % 2 else piece[:, cut:] for i, piece in enumerate(pieces)]
    near = jnp.concatenate([jnp.concatenate(x, axis=0) for x in (mine, other)], axis=1)
    rows = jnp.concatenate([near, swapped(near, "mp", 1)], axis=0)
    return rows[:, :cut], rows[:, cut:]


def shards(
    tokens, in_weight, short_taps, carry_rows, pole_rates, residues, carry_state, skip_gain, groups
):
    f32, bf16 = jnp.float32, jnp.bfloat16
    seq, mp = lax.axis_size("seq"), lax.axis_size("mp")
    line = seq // 2
    here, shard = lax.axis_index("seq"), lax.axis_index("mp")
    side = here % 2
    depth, _, columns = in_weight.shape
    assert seq & (seq - 1) == 0 and line == mp and tokens.shape[1] == 2 * depth
    width = columns // seq

    by_branch = in_weight.transpose(1, 0, 2)
    half = columns // 2

    def columns_of(weights, j, upper, start=0, rows=depth):
        return lax.dynamic_slice(weights, (j, start, upper * half), (1, rows, half))[0]

    def turn(detour):
        return [
            ((2 * z + y) * mp + (m ^ detour), (2 * m + y) * mp + bits_turned(z, line))
            for z in range(line)
            for y in range(2)
            for m in range(mp)
        ]

    share = tokens.shape[0] // 2
    sided = jnp.concatenate(halves(tokens, 1, side), axis=1)
    hopped = swapped(sided[share:], "mp", mp // 2)
    early = swapped(columns_of(by_branch, 1, 1 - side, 0, depth // 2), "seq", 1)
    turned = [
        lax.ppermute(sided[:share], ("seq", "mp"), turn(0)),
        lax.ppermute(hopped, ("seq", "mp"), turn(mp // 2)),
    ]
    crossed = [swapped(piece, "seq", 1) for piece in turned]
    parts = [plane_rows(*pair) for pair in zip(turned, crossed)]

    by_branch, *_ = lax.optimization_barrier((by_branch, *crossed))
    late = swapped(columns_of(by_branch, 1, 1 - side, depth // 2, depth // 2), "seq", 1)
    arrived = [None, jnp.concatenate([early, late], axis=0)]
    arrived.append(swapped(columns_of(by_branch, 2, 1 - side), "seq", 1))

    def bit_of(bit):
        return here // bit % 2

    def send(total, bit, groups=1):
        goes = picked(total, groups, 1 - bit_of(bit)).astype(bf16)
        if bit == 1:
            pairs = goes.reshape(line, 2, share, goes.shape[1])
            goes = jnp.stack([pairs[:, 1], pairs[:, 0]], axis=1).reshape(goes.shape)
        return picked(total, groups, bit_of(bit)), swapped(goes, "seq", bit), goes

    sums = [[None] * 3 for _ in parts]

    waiting = []
    for rows_mine, _ in parts:
        total = jnp.dot(rows_mine, by_branch[0], preferred_element_type=f32)
        waiting.append(send(total, 2, groups=2))
    for p, (total, came, _) in enumerate(waiting):
        waiting[p] = send(total + came.astype(f32), 1)

    def planes(total, bit):
        sent = ()
        while bit < seq:
            total, came, goes = send(total, bit)
            sent, bit = (*sent, goes), 2 * bit
            if bit < seq:
                total = total + came.astype(f32)
        return (total, came), sent

    after = [goes for _, _, goes in waiting]
    for j in (1, 2):
        weights, *_ = lax.optimization_barrier((arrived[j], *after))
        after = []
        for p, (rows_mine, rows_other) in enumerate(parts):
            total = jnp.dot(
                rows_mine, columns_of(by_branch, j, side), preferred_element_type=f32
            ) + jnp.dot(rows_other, weights, preferred_element_type=f32)
            sums[p][j], sent = planes(total, 2)
            after.extend(sent)
    for p, (total, came, _) in enumerate(waiting):
        sums[p][0], _ = planes(total + came.astype(f32), 4)
    sums = [term for part in sums for pair in part for term in pair]

    first = bits_turned(here, seq) * width

    def own(array, axis):
        return lax.dynamic_slice_in_dim(array, first, width, axis)

    length = tokens.shape[0] * seq
    chan_rates, chan_res = channel_modes(own(groups, 0), pole_rates, residues)
    places = jnp.arange(seq, dtype=jnp.int32)
    holder = shard ^ bits_turned(places // 2, mp)
    token_at = 2 * bits_turned(holder, mp) + (side ^ (places % 2))
    mixed = run_mode_scan(
        token_at.astype(jnp.int32),
        sums,
        own(short_taps, 2),
        own(carry_rows, 2),
        jnp.exp(-chan_rates),
        jnp.exp(-chan_rates * (length // SUBLANES)),
        chan_res,
        own(carry_state.T, 1),
        own(skip_gain, 0)[None, :],
    )
    back = lax.all_to_all(
        mixed.reshape(seq, length // seq, width), "seq", split_axis=0, concat_axis=0, tiled=True
    )
    bits = seq.bit_length() - 1
    back = back.reshape((2,) * bits + back.shape[1:])
    return back.transpose(bits, *range(bits)[::-1], bits + 1).reshape(length // seq, columns)


def solution(mesh):
    in_specs = (
        P("seq", "mp"),
        P("seq", None, "mp"),
        P(None, None, "mp"),
        P(None, None, "mp"),
        P(),
        P(),
        P("mp", None),
        P("mp"),
        P("mp"),
    )
    out_specs = P("seq", "mp")
    return jax.shard_map(shards, mesh=mesh, in_specs=in_specs, out_specs=out_specs, check_vma=False)
```

```python
import jax
import jax.numpy as jnp
from jax import lax
from jax.experimental import pallas as pl
from jax.experimental.pallas import tpu as pltpu
from jax.sharding import PartitionSpec as P

LANES = 128
SUBLANES = 8


def mode_scan(token_at, *refs):
    *sums, taps, carry, decay, decay_chunk, weight, state, skip = refs[:-7]
    out, ext, query, gated, mixed, ends, starts = refs[-7:]
    length = query.shape[0]
    blocks = token_at.shape[0]
    parts = len(sums) // 6
    rows = length // blocks
    share = rows // parts
    steps = length // SUBLANES
    modes = decay.shape[0]
    f32 = jnp.float32
    for j in range(3):
        ext[j, SUBLANES - 2 : SUBLANES, :] = carry[:, j, :].astype(f32)
    for part, p in [(part, p) for part in range(parts) for p in range(blocks)]:
        src = pl.ds(p * share, share)
        dst = pl.ds(
            pl.multiple_of(token_at[p] * rows + part * share + SUBLANES, SUBLANES), share
        )
        for j in range(3):
            own, other = sums[2 * (3 * part + j)], sums[2 * (3 * part + j) + 1]
            total = own[src, :] + other[src, :].astype(f32)
            ext[j, dst, :] = total.astype(jnp.bfloat16).astype(f32)
    for t in range(blocks):
        mix = []
        for j in range(3):
            acc = taps[0, j : j + 1, :] * ext[j, pl.ds(SUBLANES + t * rows, rows), :]
            acc = acc + taps[1, j : j + 1, :] * ext[j, pl.ds(SUBLANES - 1 + t * rows, rows), :]
            acc = acc + taps[2, j : j + 1, :] * ext[j, pl.ds(SUBLANES - 2 + t * rows, rows), :]
            mix.append(acc)
        query[pl.ds(t * rows, rows), :] = mix[0]
        gated[pl.ds(t * rows, rows), :] = (mix[1] * mix[2]).astype(jnp.bfloat16).astype(f32)

    lanes = query.shape[1]
    rates = [jnp.broadcast_to(decay[r : r + 1, :], (SUBLANES, lanes)) for r in range(modes)]

    def advance(i, held):
        x = gated[pl.ds(i, SUBLANES, stride=steps), :]
        return tuple(a * s + x for a, s in zip(rates, held))

    zero = jnp.zeros((SUBLANES, lanes), f32)
    held = lax.fori_loop(0, steps, advance, (zero,) * modes, unroll=8)
    for r in range(modes):
        ends[r] = held[r]
    start = state[...]
    for n in range(SUBLANES):
        starts[:, n, :] = start
        start = decay_chunk[...] * start + ends[:, n, :]

    weights = [jnp.broadcast_to(weight[r : r + 1, :], (SUBLANES, lanes)) for r in range(modes)]

    def emit(i, held):
        x = gated[pl.ds(i, SUBLANES, stride=steps), :]
        held = tuple(a * s + x for a, s in zip(rates, held))
        terms = [w * s for w, s in zip(weights, held)]
        while len(terms) > 1:
            terms = [sum(terms[k : k + 2]) for k in range(0, len(terms), 2)]
        mixed[pl.ds(i, SUBLANES, stride=steps), :] = terms[0]
        return held

    lax.fori_loop(0, steps, emit, tuple(starts[r] for r in range(modes)), unroll=8)
    for t in range(blocks):
        at = pl.ds(t * rows, rows)
        long_rows = mixed[at, :].astype(jnp.bfloat16).astype(f32)
        out[at, :] = (query[at, :] * (long_rows + skip[...] * gated[at, :])).astype(jnp.bfloat16)


def run_mode_scan(token_at, sums, taps, carry, decay, decay_chunk, weight, state, skip):
    blocks = token_at.shape[0]
    width = sums[0].shape[1]
    length = sum(x.shape[0] for x in sums[::6])
    lanes = -(-width // LANES) * LANES
    operands = [*sums, taps, carry, decay, decay_chunk, weight, state, skip]
    if lanes != width:
        operands = [
            jnp.pad(x, [(0, 0)] * (x.ndim - 1) + [(0, lanes - width)]) for x in operands
        ]
    modes = decay.shape[0]
    f32 = jnp.float32
    out = pl.pallas_call(
        mode_scan,
        out_shape=jax.ShapeDtypeStruct((length, lanes), jnp.bfloat16),
        in_specs=[pl.BlockSpec(memory_space=pltpu.SMEM)]
        + [pl.BlockSpec(memory_space=pltpu.VMEM)] * len(operands),
        out_specs=pl.BlockSpec(memory_space=pltpu.VMEM),
        scratch_shapes=[
            pltpu.VMEM((3, length + SUBLANES, lanes), f32),
            pltpu.VMEM((length, lanes), f32),
            pltpu.VMEM((length, lanes), f32),
            pltpu.VMEM((length, lanes), f32),
            pltpu.VMEM((modes, SUBLANES, lanes), f32),
            pltpu.VMEM((modes, SUBLANES, lanes), f32),
        ],
        compiler_params=pltpu.CompilerParams(vmem_limit_bytes=48 * 2**20),
        cost_estimate=pl.CostEstimate(
            flops=6 * modes * length * lanes, bytes_accessed=40 * length * lanes, transcendentals=0
        ),
    )(token_at, *operands)
    return out[:, :width]


def channel_modes(chan_groups, pole_rates, residues):
    highest = lax.Precision.HIGHEST
    one_hot = (
        jnp.arange(pole_rates.shape[0], dtype=jnp.int32)[:, None] == chan_groups[None, :]
    ).astype(jnp.float32)
    chan_rates = jnp.dot(pole_rates.T, one_hot, precision=highest)
    chan_res = jnp.dot(residues.T, one_hot, precision=highest)
    return (chan_rates, chan_res)


def bits_turned(index, count):
    turned, bit = index * 0, 1
    while bit < count:
        turned = turned * 2 + index // bit % 2
        bit *= 2
    return turned


def swapped(array, axis, bit):
    return lax.ppermute(array, axis, [(i, i ^ bit) for i in range(lax.axis_size(axis))])


def halves(array, axis, upper):
    half = array.shape[axis] // 2
    stays = lax.dynamic_slice_in_dim(array, upper * half, half, axis)
    goes = lax.dynamic_slice_in_dim(array, (1 - upper) * half, half, axis)
    return stays, goes


def plane_rows(turned, crossed):
    pieces, bit = [turned, crossed], lax.axis_size("mp") // 2
    while bit > 1:
        pieces = pieces + [swapped(piece, "mp", bit) for piece in pieces]
        bit //= 2
    cut = turned.shape[1] // 2
    mine = [piece[:, cut:] if i % 2 else piece[:, :cut] for i, piece in enumerate(pieces)]
    other = [piece[:, :cut] if i % 2 else piece[:, cut:] for i, piece in enumerate(pieces)]
    near = jnp.concatenate([jnp.concatenate(x, axis=0) for x in (mine, other)], axis=1)
    rows = jnp.concatenate([near, swapped(near, "mp", 1)], axis=0)
    return rows[:, :cut], rows[:, cut:]


def shards(
    tokens, in_weight, short_taps, carry_rows, pole_rates, residues, carry_state, skip_gain, groups
):
    f32, bf16 = jnp.float32, jnp.bfloat16
    seq, mp = lax.axis_size("seq"), lax.axis_size("mp")
    line = seq // 2
    here, shard = lax.axis_index("seq"), lax.axis_index("mp")
    side = here % 2
    depth, _, columns = in_weight.shape
    assert seq & (seq - 1) == 0 and line == mp and tokens.shape[1] == 2 * depth
    width = columns // seq

    by_branch = in_weight.transpose(1, 0, 2)
    half = columns // 2

    def columns_of(weights, j, upper):
        return lax.dynamic_slice(weights, (j, 0, upper * half), (1, depth, half))[0]

    arrived = [swapped(columns_of(by_branch, 0, 1 - side), "seq", 1)]

    turn = [
        ((2 * z + y) * mp + m, (2 * m + y) * mp + bits_turned(z, line))
        for z in range(line)
        for y in range(2)
        for m in range(mp)
    ]
    share = tokens.shape[0] // 2
    sided = jnp.concatenate(halves(tokens, 1, side), axis=1)
    turned = [
        lax.ppermute(piece, ("seq", "mp"), turn) for piece in (sided[:share], sided[share:])
    ]
    by_branch, _ = lax.optimization_barrier((by_branch, turned[1]))
    arrived.append(swapped(columns_of(by_branch, 1, 1 - side), "seq", 1))
    crossed = [swapped(piece, "seq", 1) for piece in turned]
    parts = [plane_rows(*pair) for pair in zip(turned, crossed)]

    def send(total, bit):
        stays, goes = halves(total, 1, here // bit % 2)
        goes = goes.astype(bf16)
        if bit == 1:
            pairs = goes.reshape(line, 2, share, goes.shape[1])
            goes = jnp.stack([pairs[:, 1], pairs[:, 0]], axis=1).reshape(goes.shape)
        return stays, swapped(goes, "seq", bit), goes

    def planes(total):
        sent, bit = (), 2
        while bit < seq:
            total, came, goes = send(total, bit)
            sent, bit = (*sent, goes), 2 * bit
            if bit < seq:
                total = total + came.astype(f32)
        return (total, came), sent

    waiting = []
    for rows_mine, _ in parts:
        total = jnp.dot(rows_mine, by_branch[2], preferred_element_type=f32)
        waiting.append(send(total, 1))

    sums = [[None] * 3 for _ in parts]
    after = ()
    for j in (0, 1):
        weights, *_ = lax.optimization_barrier((arrived[j], *after))
        after = tuple(goes for _, _, goes in waiting) if j == 0 else ()
        for p, (rows_mine, rows_other) in enumerate(parts):
            total = jnp.dot(
                rows_mine, columns_of(by_branch, j, side), preferred_element_type=f32
            ) + jnp.dot(rows_other, weights, preferred_element_type=f32)
            sums[p][j], sent = planes(total)
            after = (*after, *sent)
    for p, (total, came, _) in enumerate(waiting):
        came, *_ = lax.optimization_barrier((came, *after, *(part[p][1] for part in sums)))
        sums[p][2], after = planes(total + came.astype(f32))
    sums = [term for part in sums for pair in part for term in pair]

    first = bits_turned(here, seq) * width

    def own(array, axis):
        return lax.dynamic_slice_in_dim(array, first, width, axis)

    length = tokens.shape[0] * seq
    chan_rates, chan_res = channel_modes(own(groups, 0), pole_rates, residues)
    places = jnp.arange(seq, dtype=jnp.int32)
    holder = shard ^ bits_turned(places // 2, mp)
    token_at = 2 * bits_turned(holder, mp) + (side ^ (places % 2))
    mixed = run_mode_scan(
        token_at.astype(jnp.int32),
        sums,
        own(short_taps, 2),
        own(carry_rows, 2),
        jnp.exp(-chan_rates),
        jnp.exp(-chan_rates * (length // SUBLANES)),
        chan_res,
        own(carry_state.T, 1),
        own(skip_gain, 0)[None, :],
    )
    back = lax.all_to_all(
        mixed.reshape(seq, length // seq, width), "seq", split_axis=0, concat_axis=0, tiled=True
    )
    bits = seq.bit_length() - 1
    back = back.reshape((2,) * bits + back.shape[1:])
    return back.transpose(bits, *range(bits)[::-1], bits + 1).reshape(length // seq, columns)


def solution(mesh):
    in_specs = (
        P("seq", "mp"),
        P("seq", None, "mp"),
        P(None, None, "mp"),
        P(None, None, "mp"),
        P(),
        P(),
        P("mp", None),
        P("mp"),
        P("mp"),
    )
    out_specs = P("seq", "mp")
    return jax.shard_map(shards, mesh=mesh, in_specs=in_specs, out_specs=out_specs, check_vma=False)
```

```python
import jax
import jax.numpy as jnp
from jax import lax
from jax.experimental import pallas as pl
from jax.experimental.pallas import tpu as pltpu
from jax.sharding import PartitionSpec as P

LANES = 128
SUBLANES = 8


def mode_scan(token_at, *refs):
    *sums, taps, carry, decay, decay_chunk, weight, state, skip = refs[:-7]
    out, ext, query, gated, mixed, ends, starts = refs[-7:]
    length = query.shape[0]
    blocks = token_at.shape[0]
    parts = len(sums) // 6
    rows = length // blocks
    steps = length // SUBLANES
    modes = decay.shape[0]
    f32 = jnp.float32
    for j in range(3):
        ext[j, SUBLANES - 2 : SUBLANES, :] = carry[:, j, :].astype(f32)
    for p in range(blocks):
        part, place = divmod(p, blocks // parts)
        src = pl.ds(place * rows, rows)
        dst = pl.ds(pl.multiple_of(token_at[p] * rows + SUBLANES, SUBLANES), rows)
        for j in range(3):
            own, other = sums[2 * (3 * part + j)], sums[2 * (3 * part + j) + 1]
            total = own[src, :] + other[src, :].astype(f32)
            ext[j, dst, :] = total.astype(jnp.bfloat16).astype(f32)
    for t in range(blocks):
        mix = []
        for j in range(3):
            acc = taps[0, j : j + 1, :] * ext[j, pl.ds(SUBLANES + t * rows, rows), :]
            acc = acc + taps[1, j : j + 1, :] * ext[j, pl.ds(SUBLANES - 1 + t * rows, rows), :]
            acc = acc + taps[2, j : j + 1, :] * ext[j, pl.ds(SUBLANES - 2 + t * rows, rows), :]
            mix.append(acc)
        query[pl.ds(t * rows, rows), :] = mix[0]
        gated[pl.ds(t * rows, rows), :] = (mix[1] * mix[2]).astype(jnp.bfloat16).astype(f32)

    lanes = query.shape[1]
    rates = [jnp.broadcast_to(decay[r : r + 1, :], (SUBLANES, lanes)) for r in range(modes)]

    def advance(i, held):
        x = gated[pl.ds(i, SUBLANES, stride=steps), :]
        return tuple(a * s + x for a, s in zip(rates, held))

    zero = jnp.zeros((SUBLANES, lanes), f32)
    held = lax.fori_loop(0, steps, advance, (zero,) * modes, unroll=8)
    for r in range(modes):
        ends[r] = held[r]
    start = state[...]
    for n in range(SUBLANES):
        starts[:, n, :] = start
        start = decay_chunk[...] * start + ends[:, n, :]

    weights = [jnp.broadcast_to(weight[r : r + 1, :], (SUBLANES, lanes)) for r in range(modes)]

    def emit(i, held):
        x = gated[pl.ds(i, SUBLANES, stride=steps), :]
        held = tuple(a * s + x for a, s in zip(rates, held))
        terms = [w * s for w, s in zip(weights, held)]
        while len(terms) > 1:
            terms = [sum(terms[k : k + 2]) for k in range(0, len(terms), 2)]
        mixed[pl.ds(i, SUBLANES, stride=steps), :] = terms[0]
        return held

    lax.fori_loop(0, steps, emit, tuple(starts[r] for r in range(modes)), unroll=8)
    for t in range(blocks):
        at = pl.ds(t * rows, rows)
        long_rows = mixed[at, :].astype(jnp.bfloat16).astype(f32)
        out[at, :] = (query[at, :] * (long_rows + skip[...] * gated[at, :])).astype(jnp.bfloat16)


def run_mode_scan(token_at, sums, taps, carry, decay, decay_chunk, weight, state, skip):
    blocks = token_at.shape[0]
    width = sums[0].shape[1]
    length = sum(x.shape[0] for x in sums[::6])
    lanes = -(-width // LANES) * LANES
    operands = [*sums, taps, carry, decay, decay_chunk, weight, state, skip]
    if lanes != width:
        operands = [
            jnp.pad(x, [(0, 0)] * (x.ndim - 1) + [(0, lanes - width)]) for x in operands
        ]
    modes = decay.shape[0]
    f32 = jnp.float32
    out = pl.pallas_call(
        mode_scan,
        out_shape=jax.ShapeDtypeStruct((length, lanes), jnp.bfloat16),
        in_specs=[pl.BlockSpec(memory_space=pltpu.SMEM)]
        + [pl.BlockSpec(memory_space=pltpu.VMEM)] * len(operands),
        out_specs=pl.BlockSpec(memory_space=pltpu.VMEM),
        scratch_shapes=[
            pltpu.VMEM((3, length + SUBLANES, lanes), f32),
            pltpu.VMEM((length, lanes), f32),
            pltpu.VMEM((length, lanes), f32),
            pltpu.VMEM((length, lanes), f32),
            pltpu.VMEM((modes, SUBLANES, lanes), f32),
            pltpu.VMEM((modes, SUBLANES, lanes), f32),
        ],
        compiler_params=pltpu.CompilerParams(vmem_limit_bytes=48 * 2**20),
        cost_estimate=pl.CostEstimate(
            flops=6 * modes * length * lanes, bytes_accessed=40 * length * lanes, transcendentals=0
        ),
    )(token_at, *operands)
    return out[:, :width]


def channel_modes(chan_groups, pole_rates, residues):
    highest = lax.Precision.HIGHEST
    one_hot = (
        jnp.arange(pole_rates.shape[0], dtype=jnp.int32)[:, None] == chan_groups[None, :]
    ).astype(jnp.float32)
    chan_rates = jnp.dot(pole_rates.T, one_hot, precision=highest)
    chan_res = jnp.dot(residues.T, one_hot, precision=highest)
    return (chan_rates, chan_res)


def bits_turned(index, count):
    turned, bit = index * 0, 1
    while bit < count:
        turned = turned * 2 + index // bit % 2
        bit *= 2
    return turned


def swapped(array, axis, bit):
    return lax.ppermute(array, axis, [(i, i ^ bit) for i in range(lax.axis_size(axis))])


def halves(array, axis, upper):
    half = array.shape[axis] // 2
    stays = lax.dynamic_slice_in_dim(array, upper * half, half, axis)
    goes = lax.dynamic_slice_in_dim(array, (1 - upper) * half, half, axis)
    return stays, goes


def near_rows(halves_here, crossed):
    near = []
    for mine, other in zip(halves_here, crossed[::-1]):
        pieces, bit = [mine, other], lax.axis_size("mp") // 2
        while bit > 1:
            pieces = pieces + [swapped(piece, "mp", bit) for piece in pieces]
            bit //= 2
        near.append(jnp.concatenate(pieces, axis=0))
    return near


def shards(
    tokens, in_weight, short_taps, carry_rows, pole_rates, residues, carry_state, skip_gain, groups
):
    f32, bf16 = jnp.float32, jnp.bfloat16
    seq, mp = lax.axis_size("seq"), lax.axis_size("mp")
    line = seq // 2
    here, shard = lax.axis_index("seq"), lax.axis_index("mp")
    side = here % 2
    depth, _, columns = in_weight.shape
    assert seq & (seq - 1) == 0 and line == mp and tokens.shape[1] == 2 * depth
    width = columns // seq

    by_branch = in_weight.transpose(1, 0, 2)
    half = columns // 2

    def columns_of(j, upper, part=0, count=1):
        rows = depth // count
        return lax.dynamic_slice(by_branch, (j, part * rows, upper * half), (1, rows, half))[0]

    early = swapped(columns_of(0, 1 - side, 0, 2), "seq", 1)

    turn = [
        ((2 * z + y) * mp + m, (2 * m + y) * mp + bits_turned(z, line))
        for z in range(line)
        for y in range(2)
        for m in range(mp)
    ]
    share = tokens.shape[0]
    turned = [lax.ppermute(piece, ("seq", "mp"), turn) for piece in halves(tokens, 1, side)]
    crossed = [swapped(piece, "seq", 1) for piece in turned]
    late, _ = lax.optimization_barrier((columns_of(0, 1 - side, 1, 2), crossed[0]))
    late = swapped(late, "seq", 1)
    away, _ = lax.optimization_barrier((columns_of(1, 1 - side), crossed[1]))
    near = near_rows(turned, crossed)
    late, *near = lax.optimization_barrier((late, *near))
    far = [swapped(chunk, "mp", 1) for chunk in near]
    parts = [near, far]
    arrived = [jnp.concatenate([early, late], axis=0), swapped(away, "seq", 1)]

    def send(total, bit):
        stays, goes = halves(total, 1, here // bit % 2)
        goes = goes.astype(bf16)
        if bit == 1:
            pairs = goes.reshape(-1, 2, share, goes.shape[1])
            goes = jnp.stack([pairs[:, 1], pairs[:, 0]], axis=1).reshape(goes.shape)
        return stays, swapped(goes, "seq", bit), goes

    def planes(totals, pins):
        sent, bit = [], 2
        while True:
            moves = [send(total, bit) for total in totals]
            goes = [move[2] for move in moves]
            sent, bit = sent + goes, 2 * bit
            came = [move[1] for move in moves]
            if bit == seq:
                return [(move[0], move[1]) for move in moves], came, sent
            came = lax.optimization_barrier((*came, *goes, *pins))[: len(moves)]
            totals = [move[0] + other.astype(f32) for move, other in zip(moves, came)]
            pins = ()

    waiting = []
    for rows_mine, _ in parts:
        total = jnp.dot(rows_mine, by_branch[2], preferred_element_type=f32)
        waiting.append(send(total, 1))

    sums = [[], []]
    pins, after = (), ()
    for j in (0, 1):
        weights, *_ = lax.optimization_barrier((arrived[j], *after))
        totals = [
            jnp.dot(rows_mine, columns_of(j, side), preferred_element_type=f32)
            + jnp.dot(rows_other, weights, preferred_element_type=f32)
            for rows_mine, rows_other in parts
        ]
        pairs, pins, after = planes(totals, pins)
        for p, pair in enumerate(pairs):
            sums[p].append(pair)
        if j == 0:
            after = after + [goes for _, _, goes in waiting]
    for p, (total, came, _) in enumerate(waiting):
        came, *_ = lax.optimization_barrier((came, *after))
        pairs, pins, after = planes([total + came.astype(f32)], pins)
        sums[p].append(pairs[0])
    sums = [term for part in sums for pair in part for term in pair]

    first = bits_turned(here, seq) * width

    def own(array, axis):
        return lax.dynamic_slice_in_dim(array, first, width, axis)

    length = tokens.shape[0] * seq
    chan_rates, chan_res = channel_modes(own(groups, 0), pole_rates, residues)
    places = jnp.arange(seq, dtype=jnp.int32)
    holder = shard ^ bits_turned(places // 2, mp)
    token_at = 2 * bits_turned(holder, mp) + (side ^ (places % 2))
    mixed = run_mode_scan(
        token_at.astype(jnp.int32),
        sums,
        own(short_taps, 2),
        own(carry_rows, 2),
        jnp.exp(-chan_rates),
        jnp.exp(-chan_rates * (length // SUBLANES)),
        chan_res,
        own(carry_state.T, 1),
        own(skip_gain, 0)[None, :],
    )
    back = lax.all_to_all(
        mixed.reshape(seq, length // seq, width), "seq", split_axis=0, concat_axis=0, tiled=True
    )
    bits = seq.bit_length() - 1
    back = back.reshape((2,) * bits + back.shape[1:])
    return back.transpose(bits, *range(bits)[::-1], bits + 1).reshape(length // seq, columns)


def solution(mesh):
    in_specs = (
        P("seq", "mp"),
        P("seq", None, "mp"),
        P(None, None, "mp"),
        P(None, None, "mp"),
        P(),
        P(),
        P("mp", None),
        P("mp"),
        P("mp"),
    )
    out_specs = P("seq", "mp")
    return jax.shard_map(shards, mesh=mesh, in_specs=in_specs, out_specs=out_specs, check_vma=False)
```

```python
import jax
import jax.numpy as jnp
from jax import lax
from jax.experimental import pallas as pl
from jax.experimental.pallas import tpu as pltpu
from jax.sharding import PartitionSpec as P

LANES = 128
SUBLANES = 8


def mode_scan(token_at, *refs):
    *sums, taps, carry, decay, decay_chunk, weight, state, skip = refs[:-7]
    out, ext, query, gated, mixed, ends, starts = refs[-7:]
    length = query.shape[0]
    blocks = token_at.shape[0]
    parts = len(sums) // 6
    rows = length // blocks
    steps = length // SUBLANES
    modes = decay.shape[0]
    f32 = jnp.float32
    for j in range(3):
        ext[j, SUBLANES - 2 : SUBLANES, :] = carry[:, j, :].astype(f32)
    for p in range(blocks):
        part, place = divmod(p, blocks // parts)
        src = pl.ds(place * rows, rows)
        dst = pl.ds(pl.multiple_of(token_at[p] * rows + SUBLANES, SUBLANES), rows)
        for j in range(3):
            own, other = sums[2 * (3 * part + j)], sums[2 * (3 * part + j) + 1]
            total = own[src, :] + other[src, :].astype(f32)
            ext[j, dst, :] = total.astype(jnp.bfloat16).astype(f32)
    for t in range(blocks):
        mix = []
        for j in range(3):
            acc = taps[0, j : j + 1, :] * ext[j, pl.ds(SUBLANES + t * rows, rows), :]
            acc = acc + taps[1, j : j + 1, :] * ext[j, pl.ds(SUBLANES - 1 + t * rows, rows), :]
            acc = acc + taps[2, j : j + 1, :] * ext[j, pl.ds(SUBLANES - 2 + t * rows, rows), :]
            mix.append(acc)
        query[pl.ds(t * rows, rows), :] = mix[0]
        gated[pl.ds(t * rows, rows), :] = (mix[1] * mix[2]).astype(jnp.bfloat16).astype(f32)

    lanes = query.shape[1]
    rates = [jnp.broadcast_to(decay[r : r + 1, :], (SUBLANES, lanes)) for r in range(modes)]

    def advance(i, held):
        x = gated[pl.ds(i, SUBLANES, stride=steps), :]
        return tuple(a * s + x for a, s in zip(rates, held))

    zero = jnp.zeros((SUBLANES, lanes), f32)
    held = lax.fori_loop(0, steps, advance, (zero,) * modes, unroll=8)
    for r in range(modes):
        ends[r] = held[r]
    start = state[...]
    for n in range(SUBLANES):
        starts[:, n, :] = start
        start = decay_chunk[...] * start + ends[:, n, :]

    weights = [jnp.broadcast_to(weight[r : r + 1, :], (SUBLANES, lanes)) for r in range(modes)]

    def emit(i, held):
        x = gated[pl.ds(i, SUBLANES, stride=steps), :]
        held = tuple(a * s + x for a, s in zip(rates, held))
        terms = [w * s for w, s in zip(weights, held)]
        while len(terms) > 1:
            terms = [sum(terms[k : k + 2]) for k in range(0, len(terms), 2)]
        mixed[pl.ds(i, SUBLANES, stride=steps), :] = terms[0]
        return held

    lax.fori_loop(0, steps, emit, tuple(starts[r] for r in range(modes)), unroll=8)
    for t in range(blocks):
        at = pl.ds(t * rows, rows)
        long_rows = mixed[at, :].astype(jnp.bfloat16).astype(f32)
        out[at, :] = (query[at, :] * (long_rows + skip[...] * gated[at, :])).astype(jnp.bfloat16)


def run_mode_scan(token_at, sums, taps, carry, decay, decay_chunk, weight, state, skip):
    blocks = token_at.shape[0]
    width = sums[0].shape[1]
    length = sum(x.shape[0] for x in sums[::6])
    lanes = -(-width // LANES) * LANES
    operands = [*sums, taps, carry, decay, decay_chunk, weight, state, skip]
    if lanes != width:
        operands = [
            jnp.pad(x, [(0, 0)] * (x.ndim - 1) + [(0, lanes - width)]) for x in operands
        ]
    modes = decay.shape[0]
    f32 = jnp.float32
    out = pl.pallas_call(
        mode_scan,
        out_shape=jax.ShapeDtypeStruct((length, lanes), jnp.bfloat16),
        in_specs=[pl.BlockSpec(memory_space=pltpu.SMEM)]
        + [pl.BlockSpec(memory_space=pltpu.VMEM)] * len(operands),
        out_specs=pl.BlockSpec(memory_space=pltpu.VMEM),
        scratch_shapes=[
            pltpu.VMEM((3, length + SUBLANES, lanes), f32),
            pltpu.VMEM((length, lanes), f32),
            pltpu.VMEM((length, lanes), f32),
            pltpu.VMEM((length, lanes), f32),
            pltpu.VMEM((modes, SUBLANES, lanes), f32),
            pltpu.VMEM((modes, SUBLANES, lanes), f32),
        ],
        compiler_params=pltpu.CompilerParams(vmem_limit_bytes=48 * 2**20),
        cost_estimate=pl.CostEstimate(
            flops=6 * modes * length * lanes, bytes_accessed=40 * length * lanes, transcendentals=0
        ),
    )(token_at, *operands)
    return out[:, :width]


def channel_modes(chan_groups, pole_rates, residues):
    highest = lax.Precision.HIGHEST
    one_hot = (
        jnp.arange(pole_rates.shape[0], dtype=jnp.int32)[:, None] == chan_groups[None, :]
    ).astype(jnp.float32)
    chan_rates = jnp.dot(pole_rates.T, one_hot, precision=highest)
    chan_res = jnp.dot(residues.T, one_hot, precision=highest)
    return (chan_rates, chan_res)


def bits_turned(index, count):
    turned, bit = index * 0, 1
    while bit < count:
        turned = turned * 2 + index // bit % 2
        bit *= 2
    return turned


def swapped(array, axis, bit):
    return lax.ppermute(array, axis, [(i, i ^ bit) for i in range(lax.axis_size(axis))])


def halves(array, axis, upper):
    half = array.shape[axis] // 2
    stays = lax.dynamic_slice_in_dim(array, upper * half, half, axis)
    goes = lax.dynamic_slice_in_dim(array, (1 - upper) * half, half, axis)
    return stays, goes


def near_rows(pieces, crossed):
    held = [pieces, crossed]
    bit = lax.axis_size("mp") // 2
    while bit > 1:
        held = held + [[swapped(piece, "mp", bit) for piece in pair] for pair in held]
        bit //= 2
    cut = pieces[0].shape[1] // 2
    mine = [x[:, cut:] if i % 2 else x[:, :cut] for i, pair in enumerate(held) for x in pair]
    other = [x[:, :cut] if i % 2 else x[:, cut:] for i, pair in enumerate(held) for x in pair]
    return [jnp.concatenate(mine, axis=0), jnp.concatenate(other, axis=0)]


def shards(
    tokens, in_weight, short_taps, carry_rows, pole_rates, residues, carry_state, skip_gain, groups
):
    f32, bf16 = jnp.float32, jnp.bfloat16
    seq, mp = lax.axis_size("seq"), lax.axis_size("mp")
    line = seq // 2
    here, shard = lax.axis_index("seq"), lax.axis_index("mp")
    side = here % 2
    depth, _, columns = in_weight.shape
    assert seq & (seq - 1) == 0 and line == mp and tokens.shape[1] == 2 * depth
    width = columns // seq

    by_branch = in_weight.transpose(1, 0, 2)
    half = columns // 2

    def columns_of(j, upper, part=0, count=1):
        rows = depth // count
        return lax.dynamic_slice(by_branch, (j, part * rows, upper * half), (1, rows, half))[0]

    early = swapped(columns_of(0, 1 - side, 0, 2), "seq", 1)

    top = mp // 2

    def route(turned, flipped):
        return [
            ((2 * (turned * top + r) + y) * mp + m, (2 * (m ^ flipped) + y) * mp + m // top * top + r)
            for r in range(top)
            for y in range(2)
            for m in range(mp)
        ]

    share = tokens.shape[0]
    sided = jnp.concatenate(halves(tokens, 1, side), axis=1)
    mine, other = halves(sided, 0, shard // top)
    other = swapped(other, "mp", top)
    pieces = [
        lax.ppermute(mine, ("seq", "mp"), route(t, 0))
        + lax.ppermute(other, ("seq", "mp"), route(t, top))
        for t in range(2)
    ]
    early, *pieces = lax.optimization_barrier((early, *pieces))
    crossed = [swapped(piece, "seq", 1) for piece in pieces]
    late, away, *_ = lax.optimization_barrier(
        (columns_of(0, 1 - side, 1, 2), columns_of(1, 1 - side), *crossed)
    )
    late, away = swapped(late, "seq", 1), swapped(away, "seq", 1)
    near = near_rows(pieces, crossed)
    late, *near = lax.optimization_barrier((late, *near))
    far = [swapped(chunk, "mp", 1) for chunk in near]
    parts = [near, far]
    arrived = [jnp.concatenate([early, late], axis=0), away]

    def send(total, bit):
        stays, goes = halves(total, 1, here // bit % 2)
        goes = goes.astype(bf16)
        if bit == 1:
            pairs = goes.reshape(-1, 2, share, goes.shape[1])
            goes = jnp.stack([pairs[:, 1], pairs[:, 0]], axis=1).reshape(goes.shape)
        return stays, swapped(goes, "seq", bit), goes

    def planes(totals, pins):
        sent, bit = [], 2
        while True:
            moves = [send(total, bit) for total in totals]
            goes = [move[2] for move in moves]
            sent, bit = sent + goes, 2 * bit
            came = [move[1] for move in moves]
            if bit == seq:
                return [(move[0], move[1]) for move in moves], came, sent
            came = lax.optimization_barrier((*came, *goes, *pins))[: len(moves)]
            totals = [move[0] + other.astype(f32) for move, other in zip(moves, came)]
            pins = ()

    waiting = []
    for rows_mine, _ in parts:
        total = jnp.dot(rows_mine, by_branch[2], preferred_element_type=f32)
        waiting.append(send(total, 1))

    sums = [[], []]
    pins, after = (), ()
    for j in (0, 1):
        weights, *_ = lax.optimization_barrier((arrived[j], *after))
        totals = [
            jnp.dot(rows_mine, columns_of(j, side), preferred_element_type=f32)
            + jnp.dot(rows_other, weights, preferred_element_type=f32)
            for rows_mine, rows_other in parts
        ]
        pairs, pins, after = planes(totals, pins)
        for p, pair in enumerate(pairs):
            sums[p].append(pair)
        if j == 0:
            after = after + [goes for _, _, goes in waiting]
            pins = pins + [waiting[0][1]]
    for p, (total, came, _) in enumerate(waiting):
        came, *_ = lax.optimization_barrier((came, *after))
        pairs, pins, after = planes([total + came.astype(f32)], pins)
        sums[p].append(pairs[0])
    sums = [term for part in sums for pair in part for term in pair]

    first = bits_turned(here, seq) * width

    def own(array, axis):
        return lax.dynamic_slice_in_dim(array, first, width, axis)

    length = tokens.shape[0] * seq
    chan_rates, chan_res = channel_modes(own(groups, 0), pole_rates, residues)
    places = jnp.arange(2 * seq, dtype=jnp.int32)
    holder = shard ^ bits_turned(places // 4, mp)
    owner = 2 * (places % 2 * top + holder % top) + (side ^ (places // 2 % 2))
    token_at = 2 * owner + holder // top
    mixed = run_mode_scan(
        token_at.astype(jnp.int32),
        sums,
        own(short_taps, 2),
        own(carry_rows, 2),
        jnp.exp(-chan_rates),
        jnp.exp(-chan_rates * (length // SUBLANES)),
        chan_res,
        own(carry_state.T, 1),
        own(skip_gain, 0)[None, :],
    )
    back = lax.all_to_all(
        mixed.reshape(seq, length // seq, width), "seq", split_axis=0, concat_axis=0, tiled=True
    )
    bits = seq.bit_length() - 1
    back = back.reshape((2,) * bits + back.shape[1:])
    return back.transpose(bits, *range(bits)[::-1], bits + 1).reshape(length // seq, columns)


def solution(mesh):
    in_specs = (
        P("seq", "mp"),
        P("seq", None, "mp"),
        P(None, None, "mp"),
        P(None, None, "mp"),
        P(),
        P(),
        P("mp", None),
        P("mp"),
        P("mp"),
    )
    out_specs = P("seq", "mp")
    return jax.shard_map(shards, mesh=mesh, in_specs=in_specs, out_specs=out_specs, check_vma=False)
```

```python
import jax
import jax.numpy as jnp
from jax import lax
from jax.experimental import pallas as pl
from jax.experimental.pallas import tpu as pltpu
from jax.sharding import PartitionSpec as P

LANES = 128
SUBLANES = 8


def mode_scan(token_at, *refs):
    *sums, taps, carry, decay, decay_chunk, weight, state, skip = refs[:-7]
    out, ext, query, gated, mixed, ends, starts = refs[-7:]
    length = query.shape[0]
    blocks = token_at.shape[0]
    parts = len(sums) // 6
    rows = length // blocks
    steps = length // SUBLANES
    modes = decay.shape[0]
    f32 = jnp.float32
    for j in range(3):
        ext[j, SUBLANES - 2 : SUBLANES, :] = carry[:, j, :].astype(f32)
    for p in range(blocks):
        part, place = divmod(p, blocks // parts)
        src = pl.ds(place * rows, rows)
        dst = pl.ds(pl.multiple_of(token_at[p] * rows + SUBLANES, SUBLANES), rows)
        for j in range(3):
            own, other = sums[2 * (3 * part + j)], sums[2 * (3 * part + j) + 1]
            total = own[src, :] + other[src, :].astype(f32)
            ext[j, dst, :] = total.astype(jnp.bfloat16).astype(f32)
    for t in range(blocks):
        mix = []
        for j in range(3):
            acc = taps[0, j : j + 1, :] * ext[j, pl.ds(SUBLANES + t * rows, rows), :]
            acc = acc + taps[1, j : j + 1, :] * ext[j, pl.ds(SUBLANES - 1 + t * rows, rows), :]
            acc = acc + taps[2, j : j + 1, :] * ext[j, pl.ds(SUBLANES - 2 + t * rows, rows), :]
            mix.append(acc)
        query[pl.ds(t * rows, rows), :] = mix[0]
        gated[pl.ds(t * rows, rows), :] = (mix[1] * mix[2]).astype(jnp.bfloat16).astype(f32)

    lanes = query.shape[1]
    rates = [jnp.broadcast_to(decay[r : r + 1, :], (SUBLANES, lanes)) for r in range(modes)]

    def advance(i, held):
        x = gated[pl.ds(i, SUBLANES, stride=steps), :]
        return tuple(a * s + x for a, s in zip(rates, held))

    zero = jnp.zeros((SUBLANES, lanes), f32)
    held = lax.fori_loop(0, steps, advance, (zero,) * modes, unroll=8)
    for r in range(modes):
        ends[r] = held[r]
    start = state[...]
    for n in range(SUBLANES):
        starts[:, n, :] = start
        start = decay_chunk[...] * start + ends[:, n, :]

    weights = [jnp.broadcast_to(weight[r : r + 1, :], (SUBLANES, lanes)) for r in range(modes)]

    def emit(i, held):
        x = gated[pl.ds(i, SUBLANES, stride=steps), :]
        held = tuple(a * s + x for a, s in zip(rates, held))
        terms = [w * s for w, s in zip(weights, held)]
        while len(terms) > 1:
            terms = [sum(terms[k : k + 2]) for k in range(0, len(terms), 2)]
        mixed[pl.ds(i, SUBLANES, stride=steps), :] = terms[0]
        return held

    lax.fori_loop(0, steps, emit, tuple(starts[r] for r in range(modes)), unroll=8)
    for t in range(blocks):
        at = pl.ds(t * rows, rows)
        long_rows = mixed[at, :].astype(jnp.bfloat16).astype(f32)
        out[at, :] = (query[at, :] * (long_rows + skip[...] * gated[at, :])).astype(jnp.bfloat16)


def run_mode_scan(token_at, sums, taps, carry, decay, decay_chunk, weight, state, skip):
    blocks = token_at.shape[0]
    width = sums[0].shape[1]
    length = sum(x.shape[0] for x in sums[::6])
    lanes = -(-width // LANES) * LANES
    operands = [*sums, taps, carry, decay, decay_chunk, weight, state, skip]
    if lanes != width:
        operands = [
            jnp.pad(x, [(0, 0)] * (x.ndim - 1) + [(0, lanes - width)]) for x in operands
        ]
    modes = decay.shape[0]
    f32 = jnp.float32
    out = pl.pallas_call(
        mode_scan,
        out_shape=jax.ShapeDtypeStruct((length, lanes), jnp.bfloat16),
        in_specs=[pl.BlockSpec(memory_space=pltpu.SMEM)]
        + [pl.BlockSpec(memory_space=pltpu.VMEM)] * len(operands),
        out_specs=pl.BlockSpec(memory_space=pltpu.VMEM),
        scratch_shapes=[
            pltpu.VMEM((3, length + SUBLANES, lanes), f32),
            pltpu.VMEM((length, lanes), f32),
            pltpu.VMEM((length, lanes), f32),
            pltpu.VMEM((length, lanes), f32),
            pltpu.VMEM((modes, SUBLANES, lanes), f32),
            pltpu.VMEM((modes, SUBLANES, lanes), f32),
        ],
        compiler_params=pltpu.CompilerParams(vmem_limit_bytes=48 * 2**20),
        cost_estimate=pl.CostEstimate(
            flops=6 * modes * length * lanes, bytes_accessed=40 * length * lanes, transcendentals=0
        ),
    )(token_at, *operands)
    return out[:, :width]


def channel_modes(chan_groups, pole_rates, residues):
    highest = lax.Precision.HIGHEST
    one_hot = (
        jnp.arange(pole_rates.shape[0], dtype=jnp.int32)[:, None] == chan_groups[None, :]
    ).astype(jnp.float32)
    chan_rates = jnp.dot(pole_rates.T, one_hot, precision=highest)
    chan_res = jnp.dot(residues.T, one_hot, precision=highest)
    return (chan_rates, chan_res)


def bits_turned(index, count):
    turned, bit = index * 0, 1
    while bit < count:
        turned = turned * 2 + index // bit % 2
        bit *= 2
    return turned


def swapped(array, axis, bit):
    return lax.ppermute(array, axis, [(i, i ^ bit) for i in range(lax.axis_size(axis))])


def halves(array, axis, upper):
    half = array.shape[axis] // 2
    stays = lax.dynamic_slice_in_dim(array, upper * half, half, axis)
    goes = lax.dynamic_slice_in_dim(array, (1 - upper) * half, half, axis)
    return stays, goes


def near_rows(piece, crossed):
    held = [piece, crossed]
    bit = lax.axis_size("mp") // 2
    while bit > 1:
        held = held + [swapped(x, "mp", bit) for x in held]
        bit //= 2
    cut = piece.shape[1] // 2
    mine = [x[:, cut:] if i % 2 else x[:, :cut] for i, x in enumerate(held)]
    other = [x[:, :cut] if i % 2 else x[:, cut:] for i, x in enumerate(held)]
    return [jnp.concatenate(mine, axis=0), jnp.concatenate(other, axis=0)]


def shards(
    tokens, in_weight, short_taps, carry_rows, pole_rates, residues, carry_state, skip_gain, groups
):
    f32, bf16 = jnp.float32, jnp.bfloat16
    seq, mp = lax.axis_size("seq"), lax.axis_size("mp")
    line = seq // 2
    here, shard = lax.axis_index("seq"), lax.axis_index("mp")
    side = here % 2
    depth, _, columns = in_weight.shape
    assert seq & (seq - 1) == 0 and line == mp and tokens.shape[1] == 2 * depth
    width = columns // seq

    by_branch = in_weight.transpose(1, 0, 2)
    half = columns // 2

    def columns_of(j, upper):
        return lax.dynamic_slice(by_branch, (j, 0, upper * half), (1, depth, half))[0]

    early = swapped(columns_of(0, 1 - side), "seq", 1)

    top = mp // 2

    def route(turned, flipped):
        return [
            ((2 * (turned * top + r) + y) * mp + m, (2 * (m ^ flipped) + y) * mp + m // top * top + r)
            for r in range(top)
            for y in range(2)
            for m in range(mp)
        ]

    share = tokens.shape[0]
    sided = jnp.concatenate(halves(tokens, 1, side), axis=1)
    mine, other = halves(sided, 0, shard // top)
    other = swapped(other, "mp", top)
    pieces = [
        lax.ppermute(mine, ("seq", "mp"), route(t, 0))
        + lax.ppermute(other, ("seq", "mp"), route(t, top))
        for t in range(2)
    ]
    piece = jnp.concatenate(pieces, axis=0)
    crossed = swapped(piece, "seq", 1)
    away, _ = lax.optimization_barrier((columns_of(1, 1 - side), crossed))
    away = swapped(away, "seq", 1)
    near = near_rows(piece, crossed)
    early, *near = lax.optimization_barrier((early, *near))
    far = [swapped(chunk, "mp", 1) for chunk in near]
    parts = [near, far]

    def send(totals, bit):
        moves = [halves(total, 1, here // bit % 2) for total in totals]
        goes = [move[1].astype(bf16) for move in moves]
        if bit == 1:
            goes = [x.reshape(-1, 2, share, x.shape[1]) for x in goes]
            goes = [jnp.stack([x[:, 1], x[:, 0]], axis=1) for x in goes]
            goes = [x.reshape(-1, x.shape[-1]) for x in goes]
        goes = jnp.concatenate(goes, axis=0)
        came = jnp.split(swapped(goes, "seq", bit), len(totals), axis=0)
        return [move[0] for move in moves], came, goes

    def summed(stays, came, *pins):
        came = lax.optimization_barrier((*came, *pins))[: len(stays)]
        return [x + y.astype(f32) for x, y in zip(stays, came)]

    def both(j, weights, chosen):
        return [
            jnp.dot(mine, columns_of(j, side), preferred_element_type=f32)
            + jnp.dot(other, weights, preferred_element_type=f32)
            for mine, other in chosen
        ]

    waiting = [
        send([jnp.dot(mine, by_branch[2], preferred_element_type=f32)], 1) for mine, _ in parts
    ]

    steps = seq.bit_length() - 2
    items = [("near", 0), ("far", 0), ("both", 1), ("near", 2), ("far", 2)]
    lead = [0, 0, 1, 2, 3]
    order = sorted(
        ((i, k) for i in range(len(items)) for k in range(steps)),
        key=lambda e: (lead[e[0]] + 2 * e[1], -e[1], e[0]),
    )
    state, goes_before, finals = {}, [], {}
    for slot, (i, k) in enumerate(order):
        name, j = items[i]
        chosen = {"near": parts[:1], "far": parts[1:], "both": parts}[name]
        done_before = [x for at in list(finals) if at < slot - 2 for x in finals.pop(at)]
        if k > 0:
            totals = summed(*state[i][:2], *goes_before, *done_before)
        elif j == 0:
            totals = both(0, early, chosen)
        elif j == 1:
            weights, *_ = lax.optimization_barrier((away, *goes_before, *(w[2] for w in waiting)))
            totals = both(1, weights, chosen)
        else:
            totals = summed(*waiting[name == "far"][:2], *goes_before, *done_before)
        state[i] = send(totals, 2 << k)
        goes_before = [state[i][2]]
        if k == steps - 1:
            finals[slot] = state[i][1]
    sums = [[None] * 3 for _ in parts]
    for (name, j), (stays, came, _) in zip(items, [state[i] for i in range(len(items))]):
        chosen = {"near": (0,), "far": (1,), "both": (0, 1)}[name]
        for p, x, y in zip(chosen, stays, came):
            sums[p][j] = (x, y)
    sums = [term for part in sums for pair in part for term in pair]

    first = bits_turned(here, seq) * width

    def own(array, axis):
        return lax.dynamic_slice_in_dim(array, first, width, axis)

    length = tokens.shape[0] * seq
    chan_rates, chan_res = channel_modes(own(groups, 0), pole_rates, residues)
    places = jnp.arange(2 * seq, dtype=jnp.int32)
    holder = shard ^ bits_turned(places // 4, mp)
    owner = 2 * (places % 2 * top + holder % top) + (side ^ (places // 2 % 2))
    token_at = 2 * owner + holder // top
    mixed = run_mode_scan(
        token_at.astype(jnp.int32),
        sums,
        own(short_taps, 2),
        own(carry_rows, 2),
        jnp.exp(-chan_rates),
        jnp.exp(-chan_rates * (length // SUBLANES)),
        chan_res,
        own(carry_state.T, 1),
        own(skip_gain, 0)[None, :],
    )
    back = lax.all_to_all(
        mixed.reshape(seq, length // seq, width), "seq", split_axis=0, concat_axis=0, tiled=True
    )
    bits = seq.bit_length() - 1
    back = back.reshape((2,) * bits + back.shape[1:])
    return back.transpose(bits, *range(bits)[::-1], bits + 1).reshape(length // seq, columns)


def solution(mesh):
    in_specs = (
        P("seq", "mp"),
        P("seq", None, "mp"),
        P(None, None, "mp"),
        P(None, None, "mp"),
        P(),
        P(),
        P("mp", None),
        P("mp"),
        P("mp"),
    )
    out_specs = P("seq", "mp")
    return jax.shard_map(shards, mesh=mesh, in_specs=in_specs, out_specs=out_specs, check_vma=False)
```

```python
import jax
import jax.numpy as jnp
from jax import lax
from jax.experimental import pallas as pl
from jax.experimental.pallas import tpu as pltpu
from jax.sharding import PartitionSpec as P

LANES = 128
SUBLANES = 8


def mode_scan(token_at, *refs):
    *sums, taps, carry, decay, decay_chunk, weight, state, skip = refs[:-7]
    out, ext, query, gated, mixed, ends, starts = refs[-7:]
    length = query.shape[0]
    blocks = token_at.shape[0]
    parts = len(sums) // 6
    rows = length // blocks
    steps = length // SUBLANES
    modes = decay.shape[0]
    f32 = jnp.float32
    for j in range(3):
        ext[j, SUBLANES - 2 : SUBLANES, :] = carry[:, j, :].astype(f32)
    for p in range(blocks):
        part, place = divmod(p, blocks // parts)
        src = pl.ds(place * rows, rows)
        dst = pl.ds(pl.multiple_of(token_at[p] * rows + SUBLANES, SUBLANES), rows)
        for j in range(3):
            own, other = sums[2 * (3 * part + j)], sums[2 * (3 * part + j) + 1]
            total = own[src, :] + other[src, :].astype(f32)
            ext[j, dst, :] = total.astype(jnp.bfloat16).astype(f32)
    for t in range(blocks):
        mix = []
        for j in range(3):
            acc = taps[0, j : j + 1, :] * ext[j, pl.ds(SUBLANES + t * rows, rows), :]
            acc = acc + taps[1, j : j + 1, :] * ext[j, pl.ds(SUBLANES - 1 + t * rows, rows), :]
            acc = acc + taps[2, j : j + 1, :] * ext[j, pl.ds(SUBLANES - 2 + t * rows, rows), :]
            mix.append(acc)
        query[pl.ds(t * rows, rows), :] = mix[0]
        gated[pl.ds(t * rows, rows), :] = (mix[1] * mix[2]).astype(jnp.bfloat16).astype(f32)

    lanes = query.shape[1]
    rates = [jnp.broadcast_to(decay[r : r + 1, :], (SUBLANES, lanes)) for r in range(modes)]

    def advance(i, held):
        x = gated[pl.ds(i, SUBLANES, stride=steps), :]
        return tuple(a * s + x for a, s in zip(rates, held))

    zero = jnp.zeros((SUBLANES, lanes), f32)
    held = lax.fori_loop(0, steps, advance, (zero,) * modes, unroll=8)
    for r in range(modes):
        ends[r] = held[r]
    start = state[...]
    for n in range(SUBLANES):
        starts[:, n, :] = start
        start = decay_chunk[...] * start + ends[:, n, :]

    weights = [jnp.broadcast_to(weight[r : r + 1, :], (SUBLANES, lanes)) for r in range(modes)]

    def emit(i, held):
        x = gated[pl.ds(i, SUBLANES, stride=steps), :]
        held = tuple(a * s + x for a, s in zip(rates, held))
        terms = [w * s for w, s in zip(weights, held)]
        while len(terms) > 1:
            terms = [sum(terms[k : k + 2]) for k in range(0, len(terms), 2)]
        mixed[pl.ds(i, SUBLANES, stride=steps), :] = terms[0]
        return held

    lax.fori_loop(0, steps, emit, tuple(starts[r] for r in range(modes)), unroll=8)
    for t in range(blocks):
        at = pl.ds(t * rows, rows)
        long_rows = mixed[at, :].astype(jnp.bfloat16).astype(f32)
        out[at, :] = (query[at, :] * (long_rows + skip[...] * gated[at, :])).astype(jnp.bfloat16)


def run_mode_scan(token_at, sums, taps, carry, decay, decay_chunk, weight, state, skip):
    blocks = token_at.shape[0]
    width = sums[0].shape[1]
    length = sum(x.shape[0] for x in sums[::6])
    lanes = -(-width // LANES) * LANES
    operands = [*sums, taps, carry, decay, decay_chunk, weight, state, skip]
    if lanes != width:
        operands = [
            jnp.pad(x, [(0, 0)] * (x.ndim - 1) + [(0, lanes - width)]) for x in operands
        ]
    modes = decay.shape[0]
    f32 = jnp.float32
    out = pl.pallas_call(
        mode_scan,
        out_shape=jax.ShapeDtypeStruct((length, lanes), jnp.bfloat16),
        in_specs=[pl.BlockSpec(memory_space=pltpu.SMEM)]
        + [pl.BlockSpec(memory_space=pltpu.VMEM)] * len(operands),
        out_specs=pl.BlockSpec(memory_space=pltpu.VMEM),
        scratch_shapes=[
            pltpu.VMEM((3, length + SUBLANES, lanes), f32),
            pltpu.VMEM((length, lanes), f32),
            pltpu.VMEM((length, lanes), f32),
            pltpu.VMEM((length, lanes), f32),
            pltpu.VMEM((modes, SUBLANES, lanes), f32),
            pltpu.VMEM((modes, SUBLANES, lanes), f32),
        ],
        compiler_params=pltpu.CompilerParams(vmem_limit_bytes=48 * 2**20),
        cost_estimate=pl.CostEstimate(
            flops=6 * modes * length * lanes, bytes_accessed=40 * length * lanes, transcendentals=0
        ),
    )(token_at, *operands)
    return out[:, :width]


def channel_modes(chan_groups, pole_rates, residues):
    highest = lax.Precision.HIGHEST
    one_hot = (
        jnp.arange(pole_rates.shape[0], dtype=jnp.int32)[:, None] == chan_groups[None, :]
    ).astype(jnp.float32)
    chan_rates = jnp.dot(pole_rates.T, one_hot, precision=highest)
    chan_res = jnp.dot(residues.T, one_hot, precision=highest)
    return (chan_rates, chan_res)


def bits_turned(index, count):
    turned, bit = index * 0, 1
    while bit < count:
        turned = turned * 2 + index // bit % 2
        bit *= 2
    return turned


def swapped(array, axis, bit):
    return lax.ppermute(array, axis, [(i, i ^ bit) for i in range(lax.axis_size(axis))])


def halves(array, axis, upper):
    half = array.shape[axis] // 2
    stays = lax.dynamic_slice_in_dim(array, upper * half, half, axis)
    goes = lax.dynamic_slice_in_dim(array, (1 - upper) * half, half, axis)
    return stays, goes


def near_rows(piece, crossed):
    held = [piece, crossed]
    bit = lax.axis_size("mp") // 2
    while bit > 1:
        held = held + [swapped(x, "mp", bit) for x in held]
        bit //= 2
    cut = piece.shape[1] // 2
    mine = [x[:, cut:] if i % 2 else x[:, :cut] for i, x in enumerate(held)]
    other = [x[:, :cut] if i % 2 else x[:, cut:] for i, x in enumerate(held)]
    return [jnp.concatenate(mine, axis=0), jnp.concatenate(other, axis=0)]


def shards(
    tokens, in_weight, short_taps, carry_rows, pole_rates, residues, carry_state, skip_gain, groups
):
    f32, bf16 = jnp.float32, jnp.bfloat16
    seq, mp = lax.axis_size("seq"), lax.axis_size("mp")
    line = seq // 2
    here, shard = lax.axis_index("seq"), lax.axis_index("mp")
    side = here % 2
    depth, _, columns = in_weight.shape
    assert seq & (seq - 1) == 0 and line == mp and tokens.shape[1] == 2 * depth
    width = columns // seq

    by_branch = in_weight.transpose(1, 0, 2)
    half = columns // 2

    def columns_of(j, upper, part=0, count=1):
        rows = depth // count
        return lax.dynamic_slice(by_branch, (j, part * rows, upper * half), (1, rows, half))[0]

    early = swapped(columns_of(0, 1 - side, 0, 2), "seq", 1)

    top = mp // 2

    def route(turned, flipped):
        return [
            ((2 * (turned * top + r) + y) * mp + m, (2 * (m ^ flipped) + y) * mp + m // top * top + r)
            for r in range(top)
            for y in range(2)
            for m in range(mp)
        ]

    share = tokens.shape[0]
    sided = jnp.concatenate(halves(tokens, 1, side), axis=1)
    mine, other = halves(sided, 0, shard // top)
    other = swapped(other, "mp", top)
    pieces = [
        lax.ppermute(mine, ("seq", "mp"), route(t, 0))
        + lax.ppermute(other, ("seq", "mp"), route(t, top))
        for t in range(2)
    ]
    early, *pieces = lax.optimization_barrier((early, *pieces))
    piece = jnp.concatenate(pieces, axis=0)
    crossed = swapped(piece, "seq", 1)
    late, away, _ = lax.optimization_barrier(
        (columns_of(0, 1 - side, 1, 2), columns_of(1, 1 - side), crossed)
    )
    late, away = swapped(late, "seq", 1), swapped(away, "seq", 1)
    near = near_rows(piece, crossed)
    late, *near = lax.optimization_barrier((late, *near))
    early = jnp.concatenate([early, late], axis=0)
    far = [swapped(chunk, "mp", 1) for chunk in near]
    parts = [near, far]

    def send(totals, bit):
        moves = [halves(total, 1, here // bit % 2) for total in totals]
        goes = [move[1].astype(bf16) for move in moves]
        if bit == 1:
            goes = [x.reshape(-1, 2, share, x.shape[1]) for x in goes]
            goes = [jnp.stack([x[:, 1], x[:, 0]], axis=1) for x in goes]
            goes = [x.reshape(-1, x.shape[-1]) for x in goes]
        goes = jnp.concatenate(goes, axis=0)
        came = jnp.split(swapped(goes, "seq", bit), len(totals), axis=0)
        return [move[0] for move in moves], came, goes

    def summed(stays, came, *pins):
        came = lax.optimization_barrier((*came, *pins))[: len(stays)]
        return [x + y.astype(f32) for x, y in zip(stays, came)]

    def both(j, weights, chosen):
        return [
            jnp.dot(mine, columns_of(j, side), preferred_element_type=f32)
            + jnp.dot(other, weights, preferred_element_type=f32)
            for mine, other in chosen
        ]

    waiting = [
        send([jnp.dot(mine, by_branch[2], preferred_element_type=f32)], 1) for mine, _ in parts
    ]

    steps = seq.bit_length() - 2
    items = [("near", 0), ("far", 0), ("both", 1), ("near", 2), ("far", 2)]
    lead = [0, 0, 1, 2, 3]
    order = sorted(
        ((i, k) for i in range(len(items)) for k in range(steps)),
        key=lambda e: (lead[e[0]] + 2 * e[1], -e[1], e[0]),
    )
    state, goes_before, finals = {}, [], {}
    for slot, (i, k) in enumerate(order):
        name, j = items[i]
        chosen = {"near": parts[:1], "far": parts[1:], "both": parts}[name]
        done_before = [x for at in list(finals) if at < slot - 2 for x in finals.pop(at)]
        if k > 0:
            totals = summed(*state[i][:2], *goes_before, *done_before)
        elif j == 0:
            totals = both(0, early, chosen)
        elif j == 1:
            weights, *_ = lax.optimization_barrier((away, *goes_before, *(w[2] for w in waiting)))
            totals = both(1, weights, chosen)
        else:
            totals = summed(*waiting[name == "far"][:2], *goes_before, *done_before)
        state[i] = send(totals, 2 << k)
        goes_before = [state[i][2]]
        if k == steps - 1:
            finals[slot] = state[i][1]
    sums = [[None] * 3 for _ in parts]
    for (name, j), (stays, came, _) in zip(items, [state[i] for i in range(len(items))]):
        chosen = {"near": (0,), "far": (1,), "both": (0, 1)}[name]
        for p, x, y in zip(chosen, stays, came):
            sums[p][j] = (x, y)
    sums = [term for part in sums for pair in part for term in pair]

    first = bits_turned(here, seq) * width

    def own(array, axis):
        return lax.dynamic_slice_in_dim(array, first, width, axis)

    length = tokens.shape[0] * seq
    chan_rates, chan_res = channel_modes(own(groups, 0), pole_rates, residues)
    places = jnp.arange(2 * seq, dtype=jnp.int32)
    holder = shard ^ bits_turned(places // 4, mp)
    owner = 2 * (places % 2 * top + holder % top) + (side ^ (places // 2 % 2))
    token_at = 2 * owner + holder // top
    mixed = run_mode_scan(
        token_at.astype(jnp.int32),
        sums,
        own(short_taps, 2),
        own(carry_rows, 2),
        jnp.exp(-chan_rates),
        jnp.exp(-chan_rates * (length // SUBLANES)),
        chan_res,
        own(carry_state.T, 1),
        own(skip_gain, 0)[None, :],
    )
    back = lax.all_to_all(
        mixed.reshape(seq, length // seq, width), "seq", split_axis=0, concat_axis=0, tiled=True
    )
    bits = seq.bit_length() - 1
    back = back.reshape((2,) * bits + back.shape[1:])
    return back.transpose(bits, *range(bits)[::-1], bits + 1).reshape(length // seq, columns)


def solution(mesh):
    in_specs = (
        P("seq", "mp"),
        P("seq", None, "mp"),
        P(None, None, "mp"),
        P(None, None, "mp"),
        P(),
        P(),
        P("mp", None),
        P("mp"),
        P("mp"),
    )
    out_specs = P("seq", "mp")
    return jax.shard_map(shards, mesh=mesh, in_specs=in_specs, out_specs=out_specs, check_vma=False)
```

```python
import jax
import jax.numpy as jnp
from jax import lax
from jax.experimental import pallas as pl
from jax.experimental.pallas import tpu as pltpu
from jax.sharding import PartitionSpec as P

LANES = 128
SUBLANES = 8


def mode_scan(token_at, *refs):
    *sums, taps, carry, decay, decay_chunk, weight, state, skip = refs[:-7]
    out, ext, query, gated, mixed, ends, starts = refs[-7:]
    length = query.shape[0]
    blocks = token_at.shape[0]
    parts = len(sums) // 6
    rows = length // blocks
    steps = length // SUBLANES
    modes = decay.shape[0]
    f32 = jnp.float32
    for j in range(3):
        ext[j, SUBLANES - 2 : SUBLANES, :] = carry[:, j, :].astype(f32)
    for p in range(blocks):
        part, place = divmod(p, blocks // parts)
        src = pl.ds(place * rows, rows)
        dst = pl.ds(pl.multiple_of(token_at[p] * rows + SUBLANES, SUBLANES), rows)
        for j in range(3):
            own, other = sums[2 * (3 * part + j)], sums[2 * (3 * part + j) + 1]
            total = own[src, :] + other[src, :].astype(f32)
            ext[j, dst, :] = total.astype(jnp.bfloat16).astype(f32)
    for t in range(blocks):
        mix = []
        for j in range(3):
            acc = taps[0, j : j + 1, :] * ext[j, pl.ds(SUBLANES + t * rows, rows), :]
            acc = acc + taps[1, j : j + 1, :] * ext[j, pl.ds(SUBLANES - 1 + t * rows, rows), :]
            acc = acc + taps[2, j : j + 1, :] * ext[j, pl.ds(SUBLANES - 2 + t * rows, rows), :]
            mix.append(acc)
        query[pl.ds(t * rows, rows), :] = mix[0]
        gated[pl.ds(t * rows, rows), :] = (mix[1] * mix[2]).astype(jnp.bfloat16).astype(f32)

    lanes = query.shape[1]
    rates = [jnp.broadcast_to(decay[r : r + 1, :], (SUBLANES, lanes)) for r in range(modes)]

    def advance(i, held):
        x = gated[pl.ds(i, SUBLANES, stride=steps), :]
        return tuple(a * s + x for a, s in zip(rates, held))

    zero = jnp.zeros((SUBLANES, lanes), f32)
    held = lax.fori_loop(0, steps, advance, (zero,) * modes, unroll=8)
    for r in range(modes):
        ends[r] = held[r]
    start = state[...]
    for n in range(SUBLANES):
        starts[:, n, :] = start
        start = decay_chunk[...] * start + ends[:, n, :]

    weights = [jnp.broadcast_to(weight[r : r + 1, :], (SUBLANES, lanes)) for r in range(modes)]

    def emit(i, held):
        x = gated[pl.ds(i, SUBLANES, stride=steps), :]
        held = tuple(a * s + x for a, s in zip(rates, held))
        terms = [w * s for w, s in zip(weights, held)]
        while len(terms) > 1:
            terms = [sum(terms[k : k + 2]) for k in range(0, len(terms), 2)]
        mixed[pl.ds(i, SUBLANES, stride=steps), :] = terms[0]
        return held

    lax.fori_loop(0, steps, emit, tuple(starts[r] for r in range(modes)), unroll=8)
    for t in range(blocks):
        at = pl.ds(t * rows, rows)
        long_rows = mixed[at, :].astype(jnp.bfloat16).astype(f32)
        out[at, :] = (query[at, :] * (long_rows + skip[...] * gated[at, :])).astype(jnp.bfloat16)


def run_mode_scan(token_at, sums, taps, carry, decay, decay_chunk, weight, state, skip):
    blocks = token_at.shape[0]
    width = sums[0].shape[1]
    length = sum(x.shape[0] for x in sums[::6])
    lanes = -(-width // LANES) * LANES
    operands = [*sums, taps, carry, decay, decay_chunk, weight, state, skip]
    if lanes != width:
        operands = [
            jnp.pad(x, [(0, 0)] * (x.ndim - 1) + [(0, lanes - width)]) for x in operands
        ]
    modes = decay.shape[0]
    f32 = jnp.float32
    out = pl.pallas_call(
        mode_scan,
        out_shape=jax.ShapeDtypeStruct((length, lanes), jnp.bfloat16),
        in_specs=[pl.BlockSpec(memory_space=pltpu.SMEM)]
        + [pl.BlockSpec(memory_space=pltpu.VMEM)] * len(operands),
        out_specs=pl.BlockSpec(memory_space=pltpu.VMEM),
        scratch_shapes=[
            pltpu.VMEM((3, length + SUBLANES, lanes), f32),
            pltpu.VMEM((length, lanes), f32),
            pltpu.VMEM((length, lanes), f32),
            pltpu.VMEM((length, lanes), f32),
            pltpu.VMEM((modes, SUBLANES, lanes), f32),
            pltpu.VMEM((modes, SUBLANES, lanes), f32),
        ],
        compiler_params=pltpu.CompilerParams(vmem_limit_bytes=48 * 2**20),
        cost_estimate=pl.CostEstimate(
            flops=6 * modes * length * lanes, bytes_accessed=40 * length * lanes, transcendentals=0
        ),
    )(token_at, *operands)
    return out[:, :width]


def channel_modes(chan_groups, pole_rates, residues):
    highest = lax.Precision.HIGHEST
    one_hot = (
        jnp.arange(pole_rates.shape[0], dtype=jnp.int32)[:, None] == chan_groups[None, :]
    ).astype(jnp.float32)
    chan_rates = jnp.dot(pole_rates.T, one_hot, precision=highest)
    chan_res = jnp.dot(residues.T, one_hot, precision=highest)
    return (chan_rates, chan_res)


def bits_turned(index, count):
    turned, bit = index * 0, 1
    while bit < count:
        turned = turned * 2 + index // bit % 2
        bit *= 2
    return turned


def swapped(array, axis, bit):
    return lax.ppermute(array, axis, [(i, i ^ bit) for i in range(lax.axis_size(axis))])


def halves(array, axis, upper):
    half = array.shape[axis] // 2
    stays = lax.dynamic_slice_in_dim(array, upper * half, half, axis)
    goes = lax.dynamic_slice_in_dim(array, (1 - upper) * half, half, axis)
    return stays, goes


def near_rows(piece, crossed):
    held = [piece, crossed]
    bit = lax.axis_size("mp") // 2
    while bit > 1:
        held = held + [swapped(x, "mp", bit) for x in held]
        bit //= 2
    cut = piece.shape[1] // 2
    mine = [x[:, cut:] if i % 2 else x[:, :cut] for i, x in enumerate(held)]
    other = [x[:, :cut] if i % 2 else x[:, cut:] for i, x in enumerate(held)]
    return [jnp.concatenate(mine, axis=0), jnp.concatenate(other, axis=0)]


def shards(
    tokens, in_weight, short_taps, carry_rows, pole_rates, residues, carry_state, skip_gain, groups
):
    f32, bf16 = jnp.float32, jnp.bfloat16
    seq, mp = lax.axis_size("seq"), lax.axis_size("mp")
    line = seq // 2
    here, shard = lax.axis_index("seq"), lax.axis_index("mp")
    side = here % 2
    depth, _, columns = in_weight.shape
    assert seq & (seq - 1) == 0 and line == mp and tokens.shape[1] == 2 * depth
    width = columns // seq

    by_branch = in_weight.transpose(1, 0, 2)
    half = columns // 2

    def columns_of(j, upper):
        return lax.dynamic_slice(by_branch, (j, 0, upper * half), (1, depth, half))[0]

    early = swapped(columns_of(0, 1 - side), "seq", 1)

    top = mp // 2

    def route(turned, flipped):
        return [
            ((2 * (turned * top + r) + y) * mp + m, (2 * (m ^ flipped) + y) * mp + m // top * top + r)
            for r in range(top)
            for y in range(2)
            for m in range(mp)
        ]

    share = tokens.shape[0]
    sided = jnp.concatenate(halves(tokens, 1, side), axis=1)
    mine, other = halves(sided, 0, shard // top)
    mine, other = lax.optimization_barrier((mine, swapped(other, "mp", top)))
    pieces = [
        lax.ppermute(mine, ("seq", "mp"), route(t, 0))
        + lax.ppermute(other, ("seq", "mp"), route(t, top))
        for t in range(2)
    ]
    piece = jnp.concatenate(pieces, axis=0)
    early, crossed = lax.optimization_barrier((early, swapped(piece, "seq", 1)))
    away, _ = lax.optimization_barrier((columns_of(1, 1 - side), crossed))
    away = swapped(away, "seq", 1)
    near = near_rows(piece, crossed)
    far = [swapped(chunk, "mp", 1) for chunk in near]
    parts = [near, far]

    def send(totals, bit):
        moves = [halves(total, 1, here // bit % 2) for total in totals]
        goes = [move[1].astype(bf16) for move in moves]
        if bit == 1:
            goes = [x.reshape(-1, 2, share, x.shape[1]) for x in goes]
            goes = [jnp.stack([x[:, 1], x[:, 0]], axis=1) for x in goes]
            goes = [x.reshape(-1, x.shape[-1]) for x in goes]
        goes = jnp.concatenate(goes, axis=0)
        came = jnp.split(swapped(goes, "seq", bit), len(totals), axis=0)
        return [move[0] for move in moves], came, goes

    def summed(stays, came, *pins):
        came = lax.optimization_barrier((*came, *pins))[: len(stays)]
        return [x + y.astype(f32) for x, y in zip(stays, came)]

    def both(j, weights, chosen):
        return [
            jnp.dot(mine, columns_of(j, side), preferred_element_type=f32)
            + jnp.dot(other, weights, preferred_element_type=f32)
            for mine, other in chosen
        ]

    waiting = [
        send([jnp.dot(mine, by_branch[2], preferred_element_type=f32)], 1) for mine, _ in parts
    ]

    steps = seq.bit_length() - 2
    items = [("near", 0), ("far", 0), ("both", 1), ("near", 2), ("far", 2)]
    lead = [0, 0, 1, 2, 3]
    order = sorted(
        ((i, k) for i in range(len(items)) for k in range(steps)),
        key=lambda e: (lead[e[0]] + 2 * e[1], -e[1], e[0]),
    )
    state, goes_before, finals = {}, [], {}
    for slot, (i, k) in enumerate(order):
        name, j = items[i]
        chosen = {"near": parts[:1], "far": parts[1:], "both": parts}[name]
        done_before = [x for at in list(finals) if at < slot - 2 for x in finals.pop(at)]
        if k > 0:
            totals = summed(*state[i][:2], *goes_before, *done_before)
        elif j == 0:
            totals = both(0, early, chosen)
        elif j == 1:
            weights, *_ = lax.optimization_barrier((away, *goes_before, *(w[2] for w in waiting)))
            totals = both(1, weights, chosen)
        else:
            totals = summed(*waiting[name == "far"][:2], *goes_before, *done_before)
        state[i] = send(totals, 2 << k)
        goes_before = [state[i][2]]
        if k == steps - 1:
            finals[slot] = state[i][1]
    sums = [[None] * 3 for _ in parts]
    for (name, j), (stays, came, _) in zip(items, [state[i] for i in range(len(items))]):
        chosen = {"near": (0,), "far": (1,), "both": (0, 1)}[name]
        for p, x, y in zip(chosen, stays, came):
            sums[p][j] = (x, y)
    sums = [term for part in sums for pair in part for term in pair]

    first = bits_turned(here, seq) * width

    def own(array, axis):
        return lax.dynamic_slice_in_dim(array, first, width, axis)

    length = tokens.shape[0] * seq
    chan_rates, chan_res = channel_modes(own(groups, 0), pole_rates, residues)
    places = jnp.arange(2 * seq, dtype=jnp.int32)
    holder = shard ^ bits_turned(places // 4, mp)
    owner = 2 * (places % 2 * top + holder % top) + (side ^ (places // 2 % 2))
    token_at = 2 * owner + holder // top
    mixed = run_mode_scan(
        token_at.astype(jnp.int32),
        sums,
        own(short_taps, 2),
        own(carry_rows, 2),
        jnp.exp(-chan_rates),
        jnp.exp(-chan_rates * (length // SUBLANES)),
        chan_res,
        own(carry_state.T, 1),
        own(skip_gain, 0)[None, :],
    )
    back = lax.all_to_all(
        mixed.reshape(seq, length // seq, width), "seq", split_axis=0, concat_axis=0, tiled=True
    )
    bits = seq.bit_length() - 1
    back = back.reshape((2,) * bits + back.shape[1:])
    return back.transpose(bits, *range(bits)[::-1], bits + 1).reshape(length // seq, columns)


def solution(mesh):
    in_specs = (
        P("seq", "mp"),
        P("seq", None, "mp"),
        P(None, None, "mp"),
        P(None, None, "mp"),
        P(),
        P(),
        P("mp", None),
        P("mp"),
        P("mp"),
    )
    out_specs = P("seq", "mp")
    return jax.shard_map(shards, mesh=mesh, in_specs=in_specs, out_specs=out_specs, check_vma=False)
```

```python
import jax
import jax.numpy as jnp
from jax import lax
from jax.experimental import pallas as pl
from jax.experimental.pallas import tpu as pltpu
from jax.sharding import PartitionSpec as P

LANES = 128
SUBLANES = 8


def mode_scan(token_at, *refs):
    *sums, taps, carry, decay, decay_chunk, weight, state, skip = refs[:-7]
    out, ext, query, gated, mixed, ends, starts = refs[-7:]
    length = query.shape[0]
    blocks = token_at.shape[0]
    parts = len(sums) // 6
    rows = length // blocks
    steps = length // SUBLANES
    modes = decay.shape[0]
    f32 = jnp.float32
    for j in range(3):
        ext[j, SUBLANES - 2 : SUBLANES, :] = carry[:, j, :].astype(f32)
    for p in range(blocks):
        part, place = divmod(p, blocks // parts)
        src = pl.ds(place * rows, rows)
        dst = pl.ds(pl.multiple_of(token_at[p] * rows + SUBLANES, SUBLANES), rows)
        for j in range(3):
            own, other = sums[2 * (3 * part + j)], sums[2 * (3 * part + j) + 1]
            total = own[src, :] + other[src, :].astype(f32)
            ext[j, dst, :] = total.astype(jnp.bfloat16).astype(f32)
    for t in range(blocks):
        mix = []
        for j in range(3):
            acc = taps[0, j : j + 1, :] * ext[j, pl.ds(SUBLANES + t * rows, rows), :]
            acc = acc + taps[1, j : j + 1, :] * ext[j, pl.ds(SUBLANES - 1 + t * rows, rows), :]
            acc = acc + taps[2, j : j + 1, :] * ext[j, pl.ds(SUBLANES - 2 + t * rows, rows), :]
            mix.append(acc)
        query[pl.ds(t * rows, rows), :] = mix[0]
        gated[pl.ds(t * rows, rows), :] = (mix[1] * mix[2]).astype(jnp.bfloat16).astype(f32)

    lanes = query.shape[1]
    rates = [jnp.broadcast_to(decay[r : r + 1, :], (SUBLANES, lanes)) for r in range(modes)]

    def advance(i, held):
        x = gated[pl.ds(i, SUBLANES, stride=steps), :]
        return tuple(a * s + x for a, s in zip(rates, held))

    zero = jnp.zeros((SUBLANES, lanes), f32)
    held = lax.fori_loop(0, steps, advance, (zero,) * modes, unroll=8)
    for r in range(modes):
        ends[r] = held[r]
    start = state[...]
    for n in range(SUBLANES):
        starts[:, n, :] = start
        start = decay_chunk[...] * start + ends[:, n, :]

    weights = [jnp.broadcast_to(weight[r : r + 1, :], (SUBLANES, lanes)) for r in range(modes)]

    def emit(i, held):
        x = gated[pl.ds(i, SUBLANES, stride=steps), :]
        held = tuple(a * s + x for a, s in zip(rates, held))
        terms = [w * s for w, s in zip(weights, held)]
        while len(terms) > 1:
            terms = [sum(terms[k : k + 2]) for k in range(0, len(terms), 2)]
        mixed[pl.ds(i, SUBLANES, stride=steps), :] = terms[0]
        return held

    lax.fori_loop(0, steps, emit, tuple(starts[r] for r in range(modes)), unroll=8)
    for t in range(blocks):
        at = pl.ds(t * rows, rows)
        long_rows = mixed[at, :].astype(jnp.bfloat16).astype(f32)
        out[at, :] = (query[at, :] * (long_rows + skip[...] * gated[at, :])).astype(jnp.bfloat16)


def run_mode_scan(token_at, sums, taps, carry, decay, decay_chunk, weight, state, skip):
    blocks = token_at.shape[0]
    width = sums[0].shape[1]
    length = sum(x.shape[0] for x in sums[::6])
    lanes = -(-width // LANES) * LANES
    operands = [*sums, taps, carry, decay, decay_chunk, weight, state, skip]
    if lanes != width:
        operands = [
            jnp.pad(x, [(0, 0)] * (x.ndim - 1) + [(0, lanes - width)]) for x in operands
        ]
    modes = decay.shape[0]
    f32 = jnp.float32
    out = pl.pallas_call(
        mode_scan,
        out_shape=jax.ShapeDtypeStruct((length, lanes), jnp.bfloat16),
        in_specs=[pl.BlockSpec(memory_space=pltpu.SMEM)]
        + [pl.BlockSpec(memory_space=pltpu.VMEM)] * len(operands),
        out_specs=pl.BlockSpec(memory_space=pltpu.VMEM),
        scratch_shapes=[
            pltpu.VMEM((3, length + SUBLANES, lanes), f32),
            pltpu.VMEM((length, lanes), f32),
            pltpu.VMEM((length, lanes), f32),
            pltpu.VMEM((length, lanes), f32),
            pltpu.VMEM((modes, SUBLANES, lanes), f32),
            pltpu.VMEM((modes, SUBLANES, lanes), f32),
        ],
        compiler_params=pltpu.CompilerParams(vmem_limit_bytes=48 * 2**20),
        cost_estimate=pl.CostEstimate(
            flops=6 * modes * length * lanes, bytes_accessed=40 * length * lanes, transcendentals=0
        ),
    )(token_at, *operands)
    return out[:, :width]


def channel_modes(chan_groups, pole_rates, residues):
    highest = lax.Precision.HIGHEST
    one_hot = (
        jnp.arange(pole_rates.shape[0], dtype=jnp.int32)[:, None] == chan_groups[None, :]
    ).astype(jnp.float32)
    chan_rates = jnp.dot(pole_rates.T, one_hot, precision=highest)
    chan_res = jnp.dot(residues.T, one_hot, precision=highest)
    return (chan_rates, chan_res)


def bits_turned(index, count):
    turned, bit = index * 0, 1
    while bit < count:
        turned = turned * 2 + index // bit % 2
        bit *= 2
    return turned


def swapped(array, axis, bit):
    return lax.ppermute(array, axis, [(i, i ^ bit) for i in range(lax.axis_size(axis))])


def halves(array, axis, upper):
    half = array.shape[axis] // 2
    stays = lax.dynamic_slice_in_dim(array, upper * half, half, axis)
    goes = lax.dynamic_slice_in_dim(array, (1 - upper) * half, half, axis)
    return stays, goes


def near_rows(piece, crossed):
    held = [piece, crossed]
    bit = lax.axis_size("mp") // 2
    while bit > 1:
        held = held + [swapped(x, "mp", bit) for x in held]
        bit //= 2
    cut = piece.shape[1] // 2
    mine = [x[:, cut:] if i % 2 else x[:, :cut] for i, x in enumerate(held)]
    other = [x[:, :cut] if i % 2 else x[:, cut:] for i, x in enumerate(held)]
    return [jnp.concatenate(mine, axis=0), jnp.concatenate(other, axis=0)]


def shards(
    tokens, in_weight, short_taps, carry_rows, pole_rates, residues, carry_state, skip_gain, groups
):
    f32, bf16 = jnp.float32, jnp.bfloat16
    seq, mp = lax.axis_size("seq"), lax.axis_size("mp")
    line = seq // 2
    here, shard = lax.axis_index("seq"), lax.axis_index("mp")
    side = here % 2
    depth, _, columns = in_weight.shape
    assert seq & (seq - 1) == 0 and line == mp and tokens.shape[1] == 2 * depth
    width = columns // seq

    by_branch = in_weight.transpose(1, 0, 2)
    half = columns // 2

    def columns_of(j, upper):
        return lax.dynamic_slice(by_branch, (j, 0, upper * half), (1, depth, half))[0]

    early = swapped(columns_of(0, 1 - side), "seq", 1)

    top = mp // 2

    def route(direct):
        pairs = []
        for z in range(line):
            flipped = 0 if z // top == direct else top
            for y in range(2):
                for m in range(mp):
                    place = m // top * top + z % top
                    pairs.append(((2 * z + y) * mp + m, (2 * (m ^ flipped) + y) * mp + place))
        return pairs

    share = tokens.shape[0]
    sided = jnp.concatenate(halves(tokens, 1, side), axis=1)
    mine, other = halves(sided, 0, shard // top)
    mine, other = lax.optimization_barrier((mine, swapped(other, "mp", top)))
    upper = here // 2 // top
    moves = [
        lax.ppermute(lax.select(upper == direct, mine, other), ("seq", "mp"), route(direct))
        for direct in range(2)
    ]
    straight = upper == shard // top
    pieces = [lax.select(straight, moves[i], moves[1 - i]) for i in range(2)]
    piece = jnp.concatenate(pieces, axis=0)
    early, crossed = lax.optimization_barrier((early, swapped(piece, "seq", 1)))
    away, _ = lax.optimization_barrier((columns_of(1, 1 - side), early))
    away = swapped(away, "seq", 1)
    near = near_rows(piece, crossed)
    far = [swapped(chunk, "mp", 1) for chunk in near]
    parts = [near, far]

    def send(totals, bit):
        moves = [halves(total, 1, here // bit % 2) for total in totals]
        goes = [move[1].astype(bf16) for move in moves]
        if bit == 1:
            goes = [x.reshape(-1, 2, share, x.shape[1]) for x in goes]
            goes = [jnp.stack([x[:, 1], x[:, 0]], axis=1) for x in goes]
            goes = [x.reshape(-1, x.shape[-1]) for x in goes]
        goes = jnp.concatenate(goes, axis=0)
        came = jnp.split(swapped(goes, "seq", bit), len(totals), axis=0)
        return [move[0] for move in moves], came, goes

    def summed(stays, came, *pins):
        came = lax.optimization_barrier((*came, *pins))[: len(stays)]
        return [x + y.astype(f32) for x, y in zip(stays, came)]

    def both(j, weights, chosen):
        return [
            jnp.dot(mine, columns_of(j, side), preferred_element_type=f32)
            + jnp.dot(other, weights, preferred_element_type=f32)
            for mine, other in chosen
        ]

    waiting = [
        send([jnp.dot(mine, by_branch[2], preferred_element_type=f32)], 1) for mine, _ in parts
    ]

    steps = seq.bit_length() - 2
    items = [("near", 0), ("far", 0), ("both", 1), ("near", 2), ("far", 2)]
    lead = [0, 0, 1, 2, 3]
    order = sorted(
        ((i, k) for i in range(len(items)) for k in range(steps)),
        key=lambda e: (lead[e[0]] + 2 * e[1], -e[1], e[0]),
    )
    state, goes_before, finals = {}, [], {}
    for slot, (i, k) in enumerate(order):
        name, j = items[i]
        chosen = {"near": parts[:1], "far": parts[1:], "both": parts}[name]
        done_before = [x for at in list(finals) if at < slot - 2 for x in finals.pop(at)]
        if k > 0:
            totals = summed(*state[i][:2], *goes_before, *done_before)
        elif j == 0:
            totals = both(0, early, chosen)
        elif j == 1:
            weights, *_ = lax.optimization_barrier((away, *goes_before, *(w[2] for w in waiting)))
            totals = both(1, weights, chosen)
        else:
            totals = summed(*waiting[name == "far"][:2], *goes_before, *done_before)
        state[i] = send(totals, 2 << k)
        goes_before = [state[i][2]]
        if k == steps - 1:
            finals[slot] = state[i][1]
    sums = [[None] * 3 for _ in parts]
    for (name, j), (stays, came, _) in zip(items, [state[i] for i in range(len(items))]):
        chosen = {"near": (0,), "far": (1,), "both": (0, 1)}[name]
        for p, x, y in zip(chosen, stays, came):
            sums[p][j] = (x, y)
    sums = [term for part in sums for pair in part for term in pair]

    first = bits_turned(here, seq) * width

    def own(array, axis):
        return lax.dynamic_slice_in_dim(array, first, width, axis)

    length = tokens.shape[0] * seq
    chan_rates, chan_res = channel_modes(own(groups, 0), pole_rates, residues)
    places = jnp.arange(2 * seq, dtype=jnp.int32)
    holder = shard ^ bits_turned(places // 4, mp)
    owner = 2 * (places % 2 * top + holder % top) + (side ^ (places // 2 % 2))
    token_at = 2 * owner + holder // top
    mixed = run_mode_scan(
        token_at.astype(jnp.int32),
        sums,
        own(short_taps, 2),
        own(carry_rows, 2),
        jnp.exp(-chan_rates),
        jnp.exp(-chan_rates * (length // SUBLANES)),
        chan_res,
        own(carry_state.T, 1),
        own(skip_gain, 0)[None, :],
    )
    back = lax.all_to_all(
        mixed.reshape(seq, length // seq, width), "seq", split_axis=0, concat_axis=0, tiled=True
    )
    bits = seq.bit_length() - 1
    back = back.reshape((2,) * bits + back.shape[1:])
    return back.transpose(bits, *range(bits)[::-1], bits + 1).reshape(length // seq, columns)


def solution(mesh):
    in_specs = (
        P("seq", "mp"),
        P("seq", None, "mp"),
        P(None, None, "mp"),
        P(None, None, "mp"),
        P(),
        P(),
        P("mp", None),
        P("mp"),
        P("mp"),
    )
    out_specs = P("seq", "mp")
    return jax.shard_map(shards, mesh=mesh, in_specs=in_specs, out_specs=out_specs, check_vma=False)
```

```python
import jax
import jax.numpy as jnp
from jax import lax
from jax.experimental import pallas as pl
from jax.experimental.pallas import tpu as pltpu
from jax.sharding import PartitionSpec as P

LANES = 128
SUBLANES = 8


def mode_scan(token_at, *refs):
    *sums, taps, carry, decay, decay_chunk, weight, state, skip = refs[:-7]
    out, ext, query, gated, mixed, ends, starts = refs[-7:]
    length = query.shape[0]
    blocks = token_at.shape[0]
    parts = len(sums) // 6
    rows = length // blocks
    steps = length // SUBLANES
    modes = decay.shape[0]
    f32 = jnp.float32
    for j in range(3):
        ext[j, SUBLANES - 2 : SUBLANES, :] = carry[:, j, :].astype(f32)
    for p in range(blocks):
        part, place = divmod(p, blocks // parts)
        src = pl.ds(place * rows, rows)
        dst = pl.ds(pl.multiple_of(token_at[p] * rows + SUBLANES, SUBLANES), rows)
        for j in range(3):
            own, other = sums[2 * (3 * part + j)], sums[2 * (3 * part + j) + 1]
            total = own[src, :] + other[src, :].astype(f32)
            ext[j, dst, :] = total.astype(jnp.bfloat16).astype(f32)
    for t in range(blocks):
        mix = []
        for j in range(3):
            acc = taps[0, j : j + 1, :] * ext[j, pl.ds(SUBLANES + t * rows, rows), :]
            acc = acc + taps[1, j : j + 1, :] * ext[j, pl.ds(SUBLANES - 1 + t * rows, rows), :]
            acc = acc + taps[2, j : j + 1, :] * ext[j, pl.ds(SUBLANES - 2 + t * rows, rows), :]
            mix.append(acc)
        query[pl.ds(t * rows, rows), :] = mix[0]
        gated[pl.ds(t * rows, rows), :] = (mix[1] * mix[2]).astype(jnp.bfloat16).astype(f32)

    lanes = query.shape[1]
    rates = [jnp.broadcast_to(decay[r : r + 1, :], (SUBLANES, lanes)) for r in range(modes)]

    def advance(i, held):
        x = gated[pl.ds(i, SUBLANES, stride=steps), :]
        return tuple(a * s + x for a, s in zip(rates, held))

    zero = jnp.zeros((SUBLANES, lanes), f32)
    held = lax.fori_loop(0, steps, advance, (zero,) * modes, unroll=8)
    for r in range(modes):
        ends[r] = held[r]
    start = state[...]
    for n in range(SUBLANES):
        starts[:, n, :] = start
        start = decay_chunk[...] * start + ends[:, n, :]

    weights = [jnp.broadcast_to(weight[r : r + 1, :], (SUBLANES, lanes)) for r in range(modes)]

    def emit(i, held):
        x = gated[pl.ds(i, SUBLANES, stride=steps), :]
        held = tuple(a * s + x for a, s in zip(rates, held))
        terms = [w * s for w, s in zip(weights, held)]
        while len(terms) > 1:
            terms = [sum(terms[k : k + 2]) for k in range(0, len(terms), 2)]
        mixed[pl.ds(i, SUBLANES, stride=steps), :] = terms[0]
        return held

    lax.fori_loop(0, steps, emit, tuple(starts[r] for r in range(modes)), unroll=8)
    for t in range(blocks):
        at = pl.ds(t * rows, rows)
        long_rows = mixed[at, :].astype(jnp.bfloat16).astype(f32)
        out[at, :] = (query[at, :] * (long_rows + skip[...] * gated[at, :])).astype(jnp.bfloat16)


def run_mode_scan(token_at, sums, taps, carry, decay, decay_chunk, weight, state, skip):
    blocks = token_at.shape[0]
    width = sums[0].shape[1]
    length = sum(x.shape[0] for x in sums[::6])
    lanes = -(-width // LANES) * LANES
    operands = [*sums, taps, carry, decay, decay_chunk, weight, state, skip]
    if lanes != width:
        operands = [
            jnp.pad(x, [(0, 0)] * (x.ndim - 1) + [(0, lanes - width)]) for x in operands
        ]
    modes = decay.shape[0]
    f32 = jnp.float32
    out = pl.pallas_call(
        mode_scan,
        out_shape=jax.ShapeDtypeStruct((length, lanes), jnp.bfloat16),
        in_specs=[pl.BlockSpec(memory_space=pltpu.SMEM)]
        + [pl.BlockSpec(memory_space=pltpu.VMEM)] * len(operands),
        out_specs=pl.BlockSpec(memory_space=pltpu.VMEM),
        scratch_shapes=[
            pltpu.VMEM((3, length + SUBLANES, lanes), f32),
            pltpu.VMEM((length, lanes), f32),
            pltpu.VMEM((length, lanes), f32),
            pltpu.VMEM((length, lanes), f32),
            pltpu.VMEM((modes, SUBLANES, lanes), f32),
            pltpu.VMEM((modes, SUBLANES, lanes), f32),
        ],
        compiler_params=pltpu.CompilerParams(vmem_limit_bytes=48 * 2**20),
        cost_estimate=pl.CostEstimate(
            flops=6 * modes * length * lanes, bytes_accessed=40 * length * lanes, transcendentals=0
        ),
    )(token_at, *operands)
    return out[:, :width]


def channel_modes(chan_groups, pole_rates, residues):
    highest = lax.Precision.HIGHEST
    one_hot = (
        jnp.arange(pole_rates.shape[0], dtype=jnp.int32)[:, None] == chan_groups[None, :]
    ).astype(jnp.float32)
    chan_rates = jnp.dot(pole_rates.T, one_hot, precision=highest)
    chan_res = jnp.dot(residues.T, one_hot, precision=highest)
    return (chan_rates, chan_res)


def bits_turned(index, count):
    turned, bit = index * 0, 1
    while bit < count:
        turned = turned * 2 + index // bit % 2
        bit *= 2
    return turned


def swapped(array, axis, bit):
    return lax.ppermute(array, axis, [(i, i ^ bit) for i in range(lax.axis_size(axis))])


def halves(array, axis, upper):
    half = array.shape[axis] // 2
    stays = lax.dynamic_slice_in_dim(array, upper * half, half, axis)
    goes = lax.dynamic_slice_in_dim(array, (1 - upper) * half, half, axis)
    return stays, goes


def near_rows(piece, crossed):
    held = [piece, crossed]
    bit = lax.axis_size("mp") // 2
    while bit > 1:
        held = held + [swapped(x, "mp", bit) for x in held]
        bit //= 2
    cut = piece.shape[1] // 2
    mine = [x[:, cut:] if i % 2 else x[:, :cut] for i, x in enumerate(held)]
    other = [x[:, :cut] if i % 2 else x[:, cut:] for i, x in enumerate(held)]
    return [jnp.concatenate(mine, axis=0), jnp.concatenate(other, axis=0)]


def shards(
    tokens, in_weight, short_taps, carry_rows, pole_rates, residues, carry_state, skip_gain, groups
):
    f32, bf16 = jnp.float32, jnp.bfloat16
    seq, mp = lax.axis_size("seq"), lax.axis_size("mp")
    line = seq // 2
    here, shard = lax.axis_index("seq"), lax.axis_index("mp")
    side = here % 2
    depth, _, columns = in_weight.shape
    assert seq & (seq - 1) == 0 and line == mp and tokens.shape[1] == 2 * depth
    width = columns // seq

    by_branch = in_weight.transpose(1, 0, 2)
    half = columns // 2

    def columns_of(j, upper, start=0, stop=depth):
        rows = stop - start
        return lax.dynamic_slice(by_branch, (j, start, upper * half), (1, rows, half))[0]

    ahead = depth * 3 // 4
    early = swapped(columns_of(0, 1 - side, 0, ahead), "seq", 1)

    top = mp // 2

    def route(direct):
        pairs = []
        for z in range(line):
            flipped = 0 if z // top == direct else top
            for y in range(2):
                for m in range(mp):
                    place = m // top * top + z % top
                    pairs.append(((2 * z + y) * mp + m, (2 * (m ^ flipped) + y) * mp + place))
        return pairs

    share = tokens.shape[0]
    sided = jnp.concatenate(halves(tokens, 1, side), axis=1)
    mine, other = halves(sided, 0, shard // top)
    mine, other = lax.optimization_barrier((mine, swapped(other, "mp", top)))
    upper = here // 2 // top
    moves = [
        lax.ppermute(lax.select(upper == direct, mine, other), ("seq", "mp"), route(direct))
        for direct in range(2)
    ]
    straight = upper == shard // top
    pieces = [lax.select(straight, moves[i], moves[1 - i]) for i in range(2)]
    early, *pieces = lax.optimization_barrier((early, *pieces))
    piece = jnp.concatenate(pieces, axis=0)
    crossed = swapped(piece, "seq", 1)
    late, away, _ = lax.optimization_barrier(
        (columns_of(0, 1 - side, ahead), columns_of(1, 1 - side), crossed)
    )
    late, away = swapped(late, "seq", 1), swapped(away, "seq", 1)
    near = near_rows(piece, crossed)
    late, *near = lax.optimization_barrier((late, *near))
    early = jnp.concatenate([early, late], axis=0)
    far = [swapped(chunk, "mp", 1) for chunk in near]
    parts = [near, far]

    def send(totals, bit):
        moves = [halves(total, 1, here // bit % 2) for total in totals]
        goes = [move[1].astype(bf16) for move in moves]
        if bit == 1:
            goes = [x.reshape(-1, 2, share, x.shape[1]) for x in goes]
            goes = [jnp.stack([x[:, 1], x[:, 0]], axis=1) for x in goes]
            goes = [x.reshape(-1, x.shape[-1]) for x in goes]
        goes = jnp.concatenate(goes, axis=0)
        came = jnp.split(swapped(goes, "seq", bit), len(totals), axis=0)
        return [move[0] for move in moves], came, goes

    def summed(stays, came, *pins):
        came = lax.optimization_barrier((*came, *pins))[: len(stays)]
        return [x + y.astype(f32) for x, y in zip(stays, came)]

    def both(j, weights, chosen):
        return [
            jnp.dot(mine, columns_of(j, side), preferred_element_type=f32)
            + jnp.dot(other, weights, preferred_element_type=f32)
            for mine, other in chosen
        ]

    waiting = [
        send([jnp.dot(mine, by_branch[2], preferred_element_type=f32)], 1) for mine, _ in parts
    ]

    steps = seq.bit_length() - 2
    items = [("near", 0), ("far", 0), ("both", 1), ("near", 2), ("far", 2)]
    lead = [0, 0, 1, 2, 3]
    order = sorted(
        ((i, k) for i in range(len(items)) for k in range(steps)),
        key=lambda e: (lead[e[0]] + 2 * e[1], -e[1], e[0]),
    )
    state, goes_before, finals = {}, [], {}
    for slot, (i, k) in enumerate(order):
        name, j = items[i]
        chosen = {"near": parts[:1], "far": parts[1:], "both": parts}[name]
        done_before = [x for at in list(finals) if at < slot - 2 for x in finals.pop(at)]
        if k > 0:
            totals = summed(*state[i][:2], *goes_before, *done_before)
        elif j == 0:
            totals = both(0, early, chosen)
        elif j == 1:
            weights, *_ = lax.optimization_barrier((away, *goes_before, *(w[2] for w in waiting)))
            totals = both(1, weights, chosen)
        else:
            totals = summed(*waiting[name == "far"][:2], *goes_before, *done_before)
        state[i] = send(totals, 2 << k)
        goes_before = [state[i][2]]
        if k == steps - 1:
            finals[slot] = state[i][1]
    sums = [[None] * 3 for _ in parts]
    for (name, j), (stays, came, _) in zip(items, [state[i] for i in range(len(items))]):
        chosen = {"near": (0,), "far": (1,), "both": (0, 1)}[name]
        for p, x, y in zip(chosen, stays, came):
            sums[p][j] = (x, y)
    sums = [term for part in sums for pair in part for term in pair]

    first = bits_turned(here, seq) * width

    def own(array, axis):
        return lax.dynamic_slice_in_dim(array, first, width, axis)

    length = tokens.shape[0] * seq
    chan_rates, chan_res = channel_modes(own(groups, 0), pole_rates, residues)
    places = jnp.arange(2 * seq, dtype=jnp.int32)
    holder = shard ^ bits_turned(places // 4, mp)
    owner = 2 * (places % 2 * top + holder % top) + (side ^ (places // 2 % 2))
    token_at = 2 * owner + holder // top
    mixed = run_mode_scan(
        token_at.astype(jnp.int32),
        sums,
        own(short_taps, 2),
        own(carry_rows, 2),
        jnp.exp(-chan_rates),
        jnp.exp(-chan_rates * (length // SUBLANES)),
        chan_res,
        own(carry_state.T, 1),
        own(skip_gain, 0)[None, :],
    )
    back = lax.all_to_all(
        mixed.reshape(seq, length // seq, width), "seq", split_axis=0, concat_axis=0, tiled=True
    )
    bits = seq.bit_length() - 1
    back = back.reshape((2,) * bits + back.shape[1:])
    return back.transpose(bits, *range(bits)[::-1], bits + 1).reshape(length // seq, columns)


def solution(mesh):
    in_specs = (
        P("seq", "mp"),
        P("seq", None, "mp"),
        P(None, None, "mp"),
        P(None, None, "mp"),
        P(),
        P(),
        P("mp", None),
        P("mp"),
        P("mp"),
    )
    out_specs = P("seq", "mp")
    return jax.shard_map(shards, mesh=mesh, in_specs=in_specs, out_specs=out_specs, check_vma=False)
```

```python
import jax
import jax.numpy as jnp
from jax import lax
from jax.experimental import pallas as pl
from jax.experimental.pallas import tpu as pltpu
from jax.sharding import PartitionSpec as P

LANES = 128
SUBLANES = 8


def mode_scan(token_at, *refs):
    *sums, taps, carry, decay, decay_chunk, weight, state, skip = refs[:-7]
    out, ext, query, gated, mixed, ends, starts = refs[-7:]
    length = query.shape[0]
    blocks = token_at.shape[0]
    parts = len(sums) // 6
    rows = length // blocks
    steps = length // SUBLANES
    modes = decay.shape[0]
    f32 = jnp.float32
    for j in range(3):
        ext[j, SUBLANES - 2 : SUBLANES, :] = carry[:, j, :].astype(f32)
    for p in range(blocks):
        part, place = divmod(p, blocks // parts)
        src = pl.ds(place * rows, rows)
        dst = pl.ds(pl.multiple_of(token_at[p] * rows + SUBLANES, SUBLANES), rows)
        for j in range(3):
            own, other = sums[2 * (3 * part + j)], sums[2 * (3 * part + j) + 1]
            total = own[src, :] + other[src, :].astype(f32)
            ext[j, dst, :] = total.astype(jnp.bfloat16).astype(f32)
    for t in range(blocks):
        mix = []
        for j in range(3):
            acc = taps[0, j : j + 1, :] * ext[j, pl.ds(SUBLANES + t * rows, rows), :]
            acc = acc + taps[1, j : j + 1, :] * ext[j, pl.ds(SUBLANES - 1 + t * rows, rows), :]
            acc = acc + taps[2, j : j + 1, :] * ext[j, pl.ds(SUBLANES - 2 + t * rows, rows), :]
            mix.append(acc)
        query[pl.ds(t * rows, rows), :] = mix[0]
        gated[pl.ds(t * rows, rows), :] = (mix[1] * mix[2]).astype(jnp.bfloat16).astype(f32)

    lanes = query.shape[1]
    rates = [jnp.broadcast_to(decay[r : r + 1, :], (SUBLANES, lanes)) for r in range(modes)]

    def advance(i, held):
        x = gated[pl.ds(i, SUBLANES, stride=steps), :]
        return tuple(a * s + x for a, s in zip(rates, held))

    zero = jnp.zeros((SUBLANES, lanes), f32)
    held = lax.fori_loop(0, steps, advance, (zero,) * modes, unroll=8)
    for r in range(modes):
        ends[r] = held[r]
    start = state[...]
    for n in range(SUBLANES):
        starts[:, n, :] = start
        start = decay_chunk[...] * start + ends[:, n, :]

    weights = [jnp.broadcast_to(weight[r : r + 1, :], (SUBLANES, lanes)) for r in range(modes)]

    def emit(i, held):
        x = gated[pl.ds(i, SUBLANES, stride=steps), :]
        held = tuple(a * s + x for a, s in zip(rates, held))
        terms = [w * s for w, s in zip(weights, held)]
        while len(terms) > 1:
            terms = [sum(terms[k : k + 2]) for k in range(0, len(terms), 2)]
        mixed[pl.ds(i, SUBLANES, stride=steps), :] = terms[0]
        return held

    lax.fori_loop(0, steps, emit, tuple(starts[r] for r in range(modes)), unroll=8)
    for t in range(blocks):
        at = pl.ds(t * rows, rows)
        long_rows = mixed[at, :].astype(jnp.bfloat16).astype(f32)
        out[at, :] = (query[at, :] * (long_rows + skip[...] * gated[at, :])).astype(jnp.bfloat16)


def run_mode_scan(token_at, sums, taps, carry, decay, decay_chunk, weight, state, skip):
    blocks = token_at.shape[0]
    width = sums[0].shape[1]
    length = sum(x.shape[0] for x in sums[::6])
    lanes = -(-width // LANES) * LANES
    operands = [*sums, taps, carry, decay, decay_chunk, weight, state, skip]
    if lanes != width:
        operands = [
            jnp.pad(x, [(0, 0)] * (x.ndim - 1) + [(0, lanes - width)]) for x in operands
        ]
    modes = decay.shape[0]
    f32 = jnp.float32
    out = pl.pallas_call(
        mode_scan,
        out_shape=jax.ShapeDtypeStruct((length, lanes), jnp.bfloat16),
        in_specs=[pl.BlockSpec(memory_space=pltpu.SMEM)]
        + [pl.BlockSpec(memory_space=pltpu.VMEM)] * len(operands),
        out_specs=pl.BlockSpec(memory_space=pltpu.VMEM),
        scratch_shapes=[
            pltpu.VMEM((3, length + SUBLANES, lanes), f32),
            pltpu.VMEM((length, lanes), f32),
            pltpu.VMEM((length, lanes), f32),
            pltpu.VMEM((length, lanes), f32),
            pltpu.VMEM((modes, SUBLANES, lanes), f32),
            pltpu.VMEM((modes, SUBLANES, lanes), f32),
        ],
        compiler_params=pltpu.CompilerParams(vmem_limit_bytes=48 * 2**20),
        cost_estimate=pl.CostEstimate(
            flops=6 * modes * length * lanes, bytes_accessed=40 * length * lanes, transcendentals=0
        ),
    )(token_at, *operands)
    return out[:, :width]


def channel_modes(chan_groups, pole_rates, residues):
    highest = lax.Precision.HIGHEST
    one_hot = (
        jnp.arange(pole_rates.shape[0], dtype=jnp.int32)[:, None] == chan_groups[None, :]
    ).astype(jnp.float32)
    chan_rates = jnp.dot(pole_rates.T, one_hot, precision=highest)
    chan_res = jnp.dot(residues.T, one_hot, precision=highest)
    return (chan_rates, chan_res)


def bits_turned(index, count):
    turned, bit = index * 0, 1
    while bit < count:
        turned = turned * 2 + index // bit % 2
        bit *= 2
    return turned


def swapped(array, axis, bit):
    return lax.ppermute(array, axis, [(i, i ^ bit) for i in range(lax.axis_size(axis))])


def halves(array, axis, upper):
    half = array.shape[axis] // 2
    stays = lax.dynamic_slice_in_dim(array, upper * half, half, axis)
    goes = lax.dynamic_slice_in_dim(array, (1 - upper) * half, half, axis)
    return stays, goes


def near_rows(pieces, crossed):
    cut = pieces[0].shape[1] // 2
    held = [(False, [jnp.concatenate(pieces, axis=0)]), (True, crossed)]
    bit = lax.axis_size("mp") // 2
    while bit > 1:
        held = held + [(flip, [swapped(x, "mp", bit) for x in rows]) for flip, rows in held]
        bit //= 2
    mine = [x[:, cut:] if flip else x[:, :cut] for flip, rows in held for x in rows]
    other = [x[:, :cut] if flip else x[:, cut:] for flip, rows in held for x in rows]
    return [jnp.concatenate(mine, axis=0), jnp.concatenate(other, axis=0)]


def shards(
    tokens, in_weight, short_taps, carry_rows, pole_rates, residues, carry_state, skip_gain, groups
):
    f32, bf16 = jnp.float32, jnp.bfloat16
    seq, mp = lax.axis_size("seq"), lax.axis_size("mp")
    line = seq // 2
    here, shard = lax.axis_index("seq"), lax.axis_index("mp")
    side = here % 2
    depth, _, columns = in_weight.shape
    assert seq & (seq - 1) == 0 and line == mp and tokens.shape[1] == 2 * depth
    width = columns // seq

    by_branch = in_weight.transpose(1, 0, 2)
    half = columns // 2

    def columns_of(j, upper):
        return lax.dynamic_slice(by_branch, (j, 0, upper * half), (1, depth, half))[0]

    early = swapped(columns_of(0, 1 - side), "seq", 1)

    top = mp // 2

    def route(direct):
        pairs = []
        for z in range(line):
            flipped = 0 if z // top == direct else top
            for y in range(2):
                for m in range(mp):
                    place = m // top * top + z % top
                    pairs.append(((2 * z + y) * mp + m, (2 * (m ^ flipped) + y) * mp + place))
        return pairs

    share = tokens.shape[0]
    sided = jnp.concatenate(halves(tokens, 1, side), axis=1)
    mine, other = halves(sided, 0, shard // top)
    mine, other = lax.optimization_barrier((mine, swapped(other, "mp", top)))
    upper = here // 2 // top
    moves = [
        lax.ppermute(lax.select(upper == direct, mine, other), ("seq", "mp"), route(direct))
        for direct in range(2)
    ]
    straight = upper == shard // top
    pieces = [lax.select(straight, moves[i], moves[1 - i]) for i in range(2)]
    crossed = [swapped(piece, "seq", 1) for piece in pieces]
    away, *_ = lax.optimization_barrier((columns_of(1, 1 - side), early, crossed[0]))
    away = swapped(away, "seq", 1)
    early, crossed[0] = lax.optimization_barrier((early, crossed[0]))
    near = near_rows(pieces, crossed)
    far = [swapped(chunk, "mp", 1) for chunk in near]
    parts = [near, far]

    def send(totals, bit):
        moves = [halves(total, 1, here // bit % 2) for total in totals]
        goes = [move[1].astype(bf16) for move in moves]
        if bit == 1:
            goes = [x.reshape(-1, 2, share, x.shape[1]) for x in goes]
            goes = [jnp.stack([x[:, 1], x[:, 0]], axis=1) for x in goes]
            goes = [x.reshape(-1, x.shape[-1]) for x in goes]
        goes = jnp.concatenate(goes, axis=0)
        came = jnp.split(swapped(goes, "seq", bit), len(totals), axis=0)
        return [move[0] for move in moves], came, goes

    def summed(stays, came, *pins):
        came = lax.optimization_barrier((*came, *pins))[: len(stays)]
        return [x + y.astype(f32) for x, y in zip(stays, came)]

    def both(j, weights, chosen):
        return [
            jnp.dot(mine, columns_of(j, side), preferred_element_type=f32)
            + jnp.dot(other, weights, preferred_element_type=f32)
            for mine, other in chosen
        ]

    waiting = [
        send([jnp.dot(mine, by_branch[2], preferred_element_type=f32)], 1) for mine, _ in parts
    ]

    steps = seq.bit_length() - 2
    items = [("near", 0), ("far", 0), ("both", 1), ("near", 2), ("far", 2)]
    lead = [0, 0, 1, 2, 3]
    order = sorted(
        ((i, k) for i in range(len(items)) for k in range(steps)),
        key=lambda e: (lead[e[0]] + 2 * e[1], -e[1], e[0]),
    )
    state, goes_before, finals = {}, [], {}
    for slot, (i, k) in enumerate(order):
        name, j = items[i]
        chosen = {"near": parts[:1], "far": parts[1:], "both": parts}[name]
        done_before = [x for at in list(finals) if at < slot - 2 for x in finals.pop(at)]
        if k > 0:
            totals = summed(*state[i][:2], *goes_before, *done_before)
        elif j == 0:
            totals = both(0, early, chosen)
        elif j == 1:
            weights, *_ = lax.optimization_barrier((away, *goes_before, *(w[2] for w in waiting)))
            totals = both(1, weights, chosen)
        else:
            totals = summed(*waiting[name == "far"][:2], *goes_before, *done_before)
        state[i] = send(totals, 2 << k)
        goes_before = [state[i][2]]
        if k == steps - 1:
            finals[slot] = state[i][1]
    sums = [[None] * 3 for _ in parts]
    for (name, j), (stays, came, _) in zip(items, [state[i] for i in range(len(items))]):
        chosen = {"near": (0,), "far": (1,), "both": (0, 1)}[name]
        for p, x, y in zip(chosen, stays, came):
            sums[p][j] = (x, y)
    sums = [term for part in sums for pair in part for term in pair]

    first = bits_turned(here, seq) * width

    def own(array, axis):
        return lax.dynamic_slice_in_dim(array, first, width, axis)

    length = tokens.shape[0] * seq
    chan_rates, chan_res = channel_modes(own(groups, 0), pole_rates, residues)
    places = jnp.arange(2 * seq, dtype=jnp.int32)
    holder = shard ^ bits_turned(places // 4, mp)
    owner = 2 * (places % 2 * top + holder % top) + (side ^ (places // 2 % 2))
    token_at = 2 * owner + holder // top
    mixed = run_mode_scan(
        token_at.astype(jnp.int32),
        sums,
        own(short_taps, 2),
        own(carry_rows, 2),
        jnp.exp(-chan_rates),
        jnp.exp(-chan_rates * (length // SUBLANES)),
        chan_res,
        own(carry_state.T, 1),
        own(skip_gain, 0)[None, :],
    )
    back = lax.all_to_all(
        mixed.reshape(seq, length // seq, width), "seq", split_axis=0, concat_axis=0, tiled=True
    )
    bits = seq.bit_length() - 1
    back = back.reshape((2,) * bits + back.shape[1:])
    return back.transpose(bits, *range(bits)[::-1], bits + 1).reshape(length // seq, columns)


def solution(mesh):
    in_specs = (
        P("seq", "mp"),
        P("seq", None, "mp"),
        P(None, None, "mp"),
        P(None, None, "mp"),
        P(),
        P(),
        P("mp", None),
        P("mp"),
        P("mp"),
    )
    out_specs = P("seq", "mp")
    return jax.shard_map(shards, mesh=mesh, in_specs=in_specs, out_specs=out_specs, check_vma=False)
```

```python
import jax
import jax.numpy as jnp
from jax import lax
from jax.experimental import pallas as pl
from jax.experimental.pallas import tpu as pltpu
from jax.sharding import PartitionSpec as P

LANES = 128
SUBLANES = 8


def mode_scan(token_at, *refs):
    *sums, taps, carry, decay, decay_chunk, weight, state, skip = refs[:-7]
    out, ext, query, gated, mixed, ends, starts = refs[-7:]
    length = query.shape[0]
    blocks = token_at.shape[0]
    parts = len(sums) // 6
    rows = length // blocks
    steps = length // SUBLANES
    modes = decay.shape[0]
    f32 = jnp.float32
    for j in range(3):
        ext[j, SUBLANES - 2 : SUBLANES, :] = carry[:, j, :].astype(f32)
    places = [(q, i) for q in range(parts) for i in range(sums[6 * q].shape[0] // rows)]
    for p, (part, place) in enumerate(places):
        src = pl.ds(place * rows, rows)
        dst = pl.ds(pl.multiple_of(token_at[p] * rows + SUBLANES, SUBLANES), rows)
        for j in range(3):
            own, other = sums[2 * (3 * part + j)], sums[2 * (3 * part + j) + 1]
            total = own[src, :] + other[src, :].astype(f32)
            ext[j, dst, :] = total.astype(jnp.bfloat16).astype(f32)
    for t in range(blocks):
        mix = []
        for j in range(3):
            acc = taps[0, j : j + 1, :] * ext[j, pl.ds(SUBLANES + t * rows, rows), :]
            acc = acc + taps[1, j : j + 1, :] * ext[j, pl.ds(SUBLANES - 1 + t * rows, rows), :]
            acc = acc + taps[2, j : j + 1, :] * ext[j, pl.ds(SUBLANES - 2 + t * rows, rows), :]
            mix.append(acc)
        query[pl.ds(t * rows, rows), :] = mix[0]
        gated[pl.ds(t * rows, rows), :] = (mix[1] * mix[2]).astype(jnp.bfloat16).astype(f32)

    lanes = query.shape[1]
    rates = [jnp.broadcast_to(decay[r : r + 1, :], (SUBLANES, lanes)) for r in range(modes)]

    def advance(i, held):
        x = gated[pl.ds(i, SUBLANES, stride=steps), :]
        return tuple(a * s + x for a, s in zip(rates, held))

    zero = jnp.zeros((SUBLANES, lanes), f32)
    held = lax.fori_loop(0, steps, advance, (zero,) * modes, unroll=8)
    for r in range(modes):
        ends[r] = held[r]
    start = state[...]
    for n in range(SUBLANES):
        starts[:, n, :] = start
        start = decay_chunk[...] * start + ends[:, n, :]

    weights = [jnp.broadcast_to(weight[r : r + 1, :], (SUBLANES, lanes)) for r in range(modes)]

    def emit(i, held):
        x = gated[pl.ds(i, SUBLANES, stride=steps), :]
        held = tuple(a * s + x for a, s in zip(rates, held))
        terms = [w * s for w, s in zip(weights, held)]
        while len(terms) > 1:
            terms = [sum(terms[k : k + 2]) for k in range(0, len(terms), 2)]
        mixed[pl.ds(i, SUBLANES, stride=steps), :] = terms[0]
        return held

    lax.fori_loop(0, steps, emit, tuple(starts[r] for r in range(modes)), unroll=8)
    for t in range(blocks):
        at = pl.ds(t * rows, rows)
        long_rows = mixed[at, :].astype(jnp.bfloat16).astype(f32)
        out[at, :] = (query[at, :] * (long_rows + skip[...] * gated[at, :])).astype(jnp.bfloat16)


def run_mode_scan(token_at, sums, taps, carry, decay, decay_chunk, weight, state, skip):
    blocks = token_at.shape[0]
    width = sums[0].shape[1]
    length = sum(x.shape[0] for x in sums[::6])
    lanes = -(-width // LANES) * LANES
    operands = [*sums, taps, carry, decay, decay_chunk, weight, state, skip]
    if lanes != width:
        operands = [
            jnp.pad(x, [(0, 0)] * (x.ndim - 1) + [(0, lanes - width)]) for x in operands
        ]
    modes = decay.shape[0]
    f32 = jnp.float32
    out = pl.pallas_call(
        mode_scan,
        out_shape=jax.ShapeDtypeStruct((length, lanes), jnp.bfloat16),
        in_specs=[pl.BlockSpec(memory_space=pltpu.SMEM)]
        + [pl.BlockSpec(memory_space=pltpu.VMEM)] * len(operands),
        out_specs=pl.BlockSpec(memory_space=pltpu.VMEM),
        scratch_shapes=[
            pltpu.VMEM((3, length + SUBLANES, lanes), f32),
            pltpu.VMEM((length, lanes), f32),
            pltpu.VMEM((length, lanes), f32),
            pltpu.VMEM((length, lanes), f32),
            pltpu.VMEM((modes, SUBLANES, lanes), f32),
            pltpu.VMEM((modes, SUBLANES, lanes), f32),
        ],
        compiler_params=pltpu.CompilerParams(vmem_limit_bytes=48 * 2**20),
        cost_estimate=pl.CostEstimate(
            flops=6 * modes * length * lanes, bytes_accessed=40 * length * lanes, transcendentals=0
        ),
    )(token_at, *operands)
    return out[:, :width]


def channel_modes(chan_groups, pole_rates, residues):
    highest = lax.Precision.HIGHEST
    one_hot = (
        jnp.arange(pole_rates.shape[0], dtype=jnp.int32)[:, None] == chan_groups[None, :]
    ).astype(jnp.float32)
    chan_rates = jnp.dot(pole_rates.T, one_hot, precision=highest)
    chan_res = jnp.dot(residues.T, one_hot, precision=highest)
    return (chan_rates, chan_res)


def bits_turned(index, count):
    turned, bit = index * 0, 1
    while bit < count:
        turned = turned * 2 + index // bit % 2
        bit *= 2
    return turned


def swapped(array, axis, bit):
    return lax.ppermute(array, axis, [(i, i ^ bit) for i in range(lax.axis_size(axis))])


def halves(array, axis, upper):
    half = array.shape[axis] // 2
    stays = lax.dynamic_slice_in_dim(array, upper * half, half, axis)
    goes = lax.dynamic_slice_in_dim(array, (1 - upper) * half, half, axis)
    return stays, goes


def near_rows(piece, crossed):
    held = [piece, crossed]
    bit = lax.axis_size("mp") // 2
    while bit > 1:
        held = held + [swapped(x, "mp", bit) for x in held]
        bit //= 2
    cut = piece.shape[1] // 2
    held = [x if i % 2 == 0 else jnp.roll(x, cut, 1) for i, x in enumerate(held)]
    return jnp.concatenate(held[:-1], axis=0), held[-1]


def shards(
    tokens, in_weight, short_taps, carry_rows, pole_rates, residues, carry_state, skip_gain, groups
):
    f32, bf16 = jnp.float32, jnp.bfloat16
    seq, mp = lax.axis_size("seq"), lax.axis_size("mp")
    line = seq // 2
    here, shard = lax.axis_index("seq"), lax.axis_index("mp")
    side = here % 2
    depth, _, columns = in_weight.shape
    assert seq & (seq - 1) == 0 and line == mp and tokens.shape[1] == 2 * depth
    width = columns // seq

    by_branch = in_weight.transpose(1, 0, 2)
    half = columns // 2

    def columns_of(j, upper):
        return lax.dynamic_slice(by_branch, (j, 0, upper * half), (1, depth, half))[0]

    early = swapped(columns_of(0, 1 - side), "seq", 1)

    top = mp // 2

    def route(direct):
        pairs = []
        for z in range(line):
            flipped = 0 if z // top == direct else top
            for y in range(2):
                for m in range(mp):
                    place = m // top * top + z % top
                    pairs.append(((2 * z + y) * mp + m, (2 * (m ^ flipped) + y) * mp + place))
        return pairs

    share = tokens.shape[0]
    sided = jnp.concatenate(halves(tokens, 1, side), axis=1)
    mine, other = halves(sided, 0, shard // top)
    mine, other = lax.optimization_barrier((mine, swapped(other, "mp", top)))
    upper = here // 2 // top
    moves = [
        lax.ppermute(lax.select(upper == direct, mine, other), ("seq", "mp"), route(direct))
        for direct in range(2)
    ]
    straight = upper == shard // top
    pieces = [lax.select(straight, moves[i], moves[1 - i]) for i in range(2)]
    piece = jnp.concatenate(pieces, axis=0)
    early, crossed = lax.optimization_barrier((early, swapped(piece, "seq", 1)))
    away, _ = lax.optimization_barrier((columns_of(1, 1 - side), early))
    away = swapped(away, "seq", 1)
    def send(totals, bit):
        moves = [halves(total, 1, here // bit % 2) for total in totals]
        goes = jnp.concatenate([move[1].astype(bf16) for move in moves], axis=0)
        if bit == 1:
            pairs = goes.reshape(-1, 2, share, goes.shape[1])
            goes = jnp.stack([pairs[:, 1], pairs[:, 0]], axis=1).reshape(goes.shape)
        ends = [sum(x.shape[0] for x in totals[:i]) for i in range(1, len(totals))]
        came = jnp.split(swapped(goes, "seq", bit), ends, axis=0)
        return [move[0] for move in moves], came, goes

    def summed(stays, came, *pins):
        came = lax.optimization_barrier((*came, *pins))[: len(stays)]
        return [x + y.astype(f32) for x, y in zip(stays, came)]

    def both(j, weights, chosen):
        return [
            jnp.dot(mine, columns_of(j, side), preferred_element_type=f32)
            + jnp.dot(other, weights, preferred_element_type=f32)
            for mine, other in chosen
        ]

    near, corner = near_rows(piece, crossed)
    far = swapped(near, "mp", 1)

    def sided_rows(x):
        return x[:, :depth], x[:, depth:]

    ready = sided_rows(near)
    first_sent = send(both(0, early, [ready]), 2)
    corner, far, _ = lax.optimization_barrier((corner, far, first_sent[2]))
    parts = [ready, *(sided_rows(x) for x in (corner, far, swapped(corner, "mp", 1)))]

    waiting = {
        name: send(
            [jnp.dot(parts[p][0], by_branch[2], preferred_element_type=f32) for p in chosen], 1
        )
        for name, chosen in (("near", (0, 1)), ("far", (2, 3)))
    }

    steps = seq.bit_length() - 2
    items = [("first", 0), ("last", 0), ("all", 1), ("near", 2), ("far", 2)]
    groups_of = {"first": (0,), "last": (1, 2, 3), "all": (0, 1, 2, 3), "near": (0, 1), "far": (2, 3)}
    lead = [0, 0, 1, 2, 3]
    order = sorted(
        ((i, k) for i in range(len(items)) for k in range(steps)),
        key=lambda e: (lead[e[0]] + 2 * e[1], -e[1], e[0]),
    )
    state, goes_before, finals = {}, [], {}
    for slot, (i, k) in enumerate(order):
        name, j = items[i]
        chosen = [parts[p] for p in groups_of[name]]
        done_before = [x for at in list(finals) if at < slot - 2 for x in finals.pop(at)]
        if k > 0:
            totals = summed(*state[i][:2], *goes_before, *done_before)
        elif j == 0:
            totals = both(0, early, chosen) if i else None
        elif j == 1:
            weights, *_ = lax.optimization_barrier((away, *goes_before, *(w[2] for w in waiting.values())))
            totals = both(1, weights, chosen)
        else:
            totals = summed(*waiting[name][:2], *goes_before, *done_before)
        state[i] = send(totals, 2 << k) if totals else first_sent
        goes_before = [state[i][2]]
        if k == steps - 1:
            finals[slot] = state[i][1]
    sums = [[None] * 3 for _ in parts]
    for (name, j), (stays, came, _) in zip(items, [state[i] for i in range(len(items))]):
        for p, x, y in zip(groups_of[name], stays, came):
            sums[p][j] = (x, y)
    sums = [term for part in sums for pair in part for term in pair]

    first = bits_turned(here, seq) * width

    def own(array, axis):
        return lax.dynamic_slice_in_dim(array, first, width, axis)

    length = tokens.shape[0] * seq
    chan_rates, chan_res = channel_modes(own(groups, 0), pole_rates, residues)
    places = jnp.arange(2 * seq, dtype=jnp.int32)
    holder = shard ^ bits_turned(places // 4, mp)
    owner = 2 * (places % 2 * top + holder % top) + (side ^ (places // 2 % 2))
    token_at = 2 * owner + holder // top
    mixed = run_mode_scan(
        token_at.astype(jnp.int32),
        sums,
        own(short_taps, 2),
        own(carry_rows, 2),
        jnp.exp(-chan_rates),
        jnp.exp(-chan_rates * (length // SUBLANES)),
        chan_res,
        own(carry_state.T, 1),
        own(skip_gain, 0)[None, :],
    )
    back = lax.all_to_all(
        mixed.reshape(seq, length // seq, width), "seq", split_axis=0, concat_axis=0, tiled=True
    )
    bits = seq.bit_length() - 1
    back = back.reshape((2,) * bits + back.shape[1:])
    return back.transpose(bits, *range(bits)[::-1], bits + 1).reshape(length // seq, columns)


def solution(mesh):
    in_specs = (
        P("seq", "mp"),
        P("seq", None, "mp"),
        P(None, None, "mp"),
        P(None, None, "mp"),
        P(),
        P(),
        P("mp", None),
        P("mp"),
        P("mp"),
    )
    out_specs = P("seq", "mp")
    return jax.shard_map(shards, mesh=mesh, in_specs=in_specs, out_specs=out_specs, check_vma=False)
```
